32 devices in a mesh: row: 4 (over x, core), col: 8 (over z, y).
Axes of the slice: x: 2, y: 2, z: 4, core: 2. Of those that a mesh axis runs over, the one named last changes fastest.
Arguments:
- hamiltonian: float32 [64, 4, 128, 128], P(('row', 'col')), may hold values from -20 to 20
- block_lists: int32 [64, 4], replicated, may hold values from -1 to 63, as said below
Outputs:
- density: float32 [64, 4, 128, 128], P(('row', 'col'))
The draws below stay inside these ranges and needn't reach their ends.
Inputs may be any that keep to these rules, and one draw needn't show every extreme that they name: `block_lists`: block column j = (r * 8 + c) * 2 + s sits on grid row r, grid column c, slot s. Entry 0 is j. Entry 1 is the column of the same r and s at grid column c - 1 (cyclically), entry 2 the one at c + 1, each either present or -1, present for both ends of a link or for neither. Entry 3 is never -1: the column of the same c and s on grid row r with one bit flipped, the same bit for all rows of one grid column and slot. Some columns have all four entries, some only entries 0 and 3.
All inputs are finite; a program needn't handle non-finite values.
Results may differ from the reference program's by a relative error of at most 0.0001.
Values sent between devices are 32-bit elements; how exact they have to be, the bound alone decides.
No kernel may reach another device: no remote copies, remote signals or barrier semaphores. Data moves between devices by JAX's collectives and lax.ppermute only.
A program may use at most 64 MiB of HBM per device.

```python
import math
import jax
import jax.numpy as jnp
from jax import lax

B = 128
K = 4
COLS_DEV = 2
ITERS = 6
STEPS = 2
GRID_ROWS = 4
GRID_COLS = 8
NBLK = 64


def draw_block_lists(key, part):
    grid_rows = GRID_ROWS
    grid_cols = GRID_COLS
    slots_here = COLS_DEV
    edge_key, bit_key = jax.random.split(jax.random.fold_in(key, 7))
    link_on = jax.random.randint(edge_key, (grid_rows, grid_cols, slots_here), 0, 2)
    col_ids = jnp.arange(grid_cols, dtype=jnp.int32)[None, :, None]
    link_on = jnp.where(col_ids <= 1, 1, link_on)
    link_on = jnp.where((col_ids == 3) | (col_ids == 4), 0, link_on)
    bit_count = grid_rows.bit_length() - 1
    chosen = jax.random.randint(bit_key, (1, grid_cols, slots_here), 0, bit_count)
    row_ids = jnp.arange(grid_rows, dtype=jnp.int32)[:, None, None]
    slot_ids = jnp.arange(slots_here, dtype=jnp.int32)[None, None, :]

    def locate(row_pos, col_pos):
        return (row_pos * grid_cols + col_pos) * slots_here + slot_ids
    own_ids = locate(row_ids, col_ids)
    left_ids = jnp.where(jnp.roll(link_on, 1, axis=1) == 1, locate(row_ids, (col_ids - 1) % grid_cols), -1)
    right_ids = jnp.where(link_on == 1, locate(row_ids, (col_ids + 1) % grid_cols), -1)
    partner_ids = locate(jnp.bitwise_xor(row_ids, jnp.left_shift(jnp.int32(1), chosen)), col_ids)
    stacked = jnp.stack(jnp.broadcast_arrays(own_ids, left_ids, right_ids, partner_ids), -1)
    return stacked.reshape(NBLK, K).astype(jnp.int32)


def draw_hamiltonian(key, part):
    base_key = jax.random.fold_in(jax.random.fold_in(key, 11), 0)
    row_key = jax.random.fold_in(jax.random.fold_in(key, 11), 1)
    col_key = jax.random.fold_in(jax.random.fold_in(key, 11), 2)
    order_key = jax.random.fold_in(jax.random.fold_in(key, 11), 4)
    shape_all = (NBLK, K, B, B)
    devices = GRID_ROWS * GRID_COLS
    shuffled_rank = jax.random.permutation(order_key, devices)
    device_ids = jnp.arange(NBLK, dtype=jnp.int32) // COLS_DEV
    position = shuffled_rank[device_ids].astype(jnp.float32) / max(devices - 1, 1)
    ramp = 3.0 ** position
    values = jnp.clip(jax.random.normal(base_key, shape_all, jnp.float32), -5.0, 5.0)
    row_factor = jnp.exp(jax.random.uniform(row_key, (NBLK, K, B, 1), jnp.float32, -1.15, 1.15))
    col_factor = jnp.exp(jax.random.uniform(col_key, (NBLK, K, 1, B), jnp.float32, -1.15, 1.15))
    scaled = values * row_factor * col_factor * ramp[:, None, None, None] / math.sqrt(K * B)
    return jnp.clip(scaled, -19.5, 19.5).astype(jnp.float32)


def setup_inputs(seed: int = 0) -> dict:
    key_list = jax.random.split(jax.random.key(seed), 3)
    hamiltonian = draw_hamiltonian(jax.random.fold_in(key_list[2], 71), 0)
    block_lists = draw_block_lists(jax.random.fold_in(key_list[2], 71), 0)
    return dict(hamiltonian=hamiltonian, block_lists=block_lists)


facing = (0, 2, 1, 3)
epsilon = 1e-06

def symmetric(matrix):
    return 0.5 * (matrix + jnp.swapaxes(matrix, -1, -2))

def assemble(own_col, diagonals, face_blocks, present):
    column = 0.5 * (own_col + jnp.swapaxes(face_blocks, -1, -2)) * present[:, None, None]
    blocks = symmetric(diagonals) * present[:, None, None]
    side_len = own_col.shape[-1]
    members = own_col.shape[0]
    matrix = jnp.zeros((members, side_len, members, side_len), jnp.float32)
    matrix = matrix.at[0, :, 0, :].set(column[0])
    for position in range(1, members):
        matrix = matrix.at[position, :, 0, :].set(column[position])
        matrix = matrix.at[0, :, position, :].set(column[position].T)
        matrix = matrix.at[position, :, position, :].set(blocks[position])
    return matrix.reshape(members * side_len, members * side_len)

def sign_density(matrix, first_square, scaling, present):
    full_order = matrix.shape[0]
    identity = jnp.eye(full_order, dtype=jnp.float32)
    iterate = matrix * scaling
    square = first_square * (scaling * scaling)
    for repeat in range(ITERS):
        if repeat > 0:
            square = jnp.dot(iterate, iterate, precision=lax.Precision.HIGHEST)
        iterate = jnp.dot(iterate, 1.5 * identity - 0.5 * square, precision=lax.Precision.HIGHEST)
    central = 0.5 * (identity[:, :B] - iterate[:, :B])
    return central.reshape(K, B, B) * present[:, None, None]

def reference(hamiltonian, block_lists):
    present = (block_lists >= 0).astype(jnp.float32)
    columns = jnp.arange(NBLK, dtype=jnp.int32)
    safe_lists = jnp.where(block_lists >= 0, block_lists, columns[:, None]).astype(jnp.int32)
    face_index = jnp.array(facing, dtype=jnp.int32)
    member_ids = jnp.arange(K, dtype=jnp.int32)
    current = hamiltonian
    density = hamiltonian
    for scf_round in range(STEPS):

        def build_one(column):
            own_col = current[column]
            neighbours = current[safe_lists[column]]
            diagonals = neighbours[:, 0]
            face_blocks = neighbours[member_ids, face_index]
            return assemble(own_col, diagonals, face_blocks, present[column])

        def squares(column):
            matrix = build_one(column)
            square = jnp.dot(matrix, matrix, precision=lax.Precision.HIGHEST)
            return jnp.sum(square * square)
        largest = jnp.max(lax.map(squares, columns))
        scaling = 1.5 / jnp.sqrt(jnp.sqrt(largest + epsilon))

        def solve_one(column):
            matrix = build_one(column)
            square = jnp.dot(matrix, matrix, precision=lax.Precision.HIGHEST)
            return sign_density(matrix, square, scaling, present[column])
        density_cols = lax.map(solve_one, columns)
        density_face = density_cols[safe_lists, face_index[None, :]]
        density = 0.5 * (density_cols + jnp.swapaxes(density_face, -1, -2)) * present[:, :, None, None]
        current = hamiltonian + density
    return density
```

```python
import functools
import jax
import jax.numpy as jnp
from jax import lax
from jax.experimental import pallas as pl
from jax.experimental.pallas import tpu as pltpu
from jax.sharding import PartitionSpec as P

ITERS = 6
STEPS = 2
SIDE = 128
HALF = SIDE // 2
PACKED = HALF + 8

epsilon = 1e-06
f32 = jnp.float32
bf16 = jnp.bfloat16


def turned(block):
    return jnp.swapaxes(block, -1, -2)


def symmetric(block):
    return 0.5 * (block + turned(block))


def split(values):
    high = values.astype(bf16)
    return high, (values - high.astype(f32)).astype(bf16)


def dot(left, right):
    return lax.dot_general(left, right, (((1,), (0,)), ((), ())), preferred_element_type=f32)


def product(left, right, rows, cols):
    left_high, left_low = left[0][rows, :], left[1][rows, :]
    right_high, right_low = right[0][:, cols], right[1][:, cols]
    return dot(
        jnp.concatenate([left_high, left_low, left_high], 1),
        jnp.concatenate([right_high, right_high, right_low], 0),
    )


def upper_tiles(order):
    tile = order // 2
    for row, col in ((0, 0), (0, 1), (1, 1)):
        yield pl.ds(row * tile, tile), pl.ds(col * tile, tile), row != col


def lanes(shape):
    return lax.broadcasted_iota(jnp.int32, shape, 1)


def rows_of(shape):
    return lax.broadcasted_iota(jnp.int32, shape, 0)


def pack(block):
    shape = (HALF, SIDE)
    lower = pltpu.roll(block[HALF:, :], HALF, 1)
    body = jnp.where(lanes(shape) < rows_of(shape), lower, block[:HALF, :])
    whole = block.shape
    diagonal = jnp.sum(jnp.where(lanes(whole) == rows_of(whole), block, 0.0), 0, keepdims=True)
    return body, jnp.broadcast_to(diagonal, (PACKED - HALF, SIDE))


def unpack(body, diagonal):
    shape = (HALF, SIDE)
    lane, row = lanes(shape), rows_of(shape)
    top = jnp.where(lane == row, 0.5 * body, jnp.where(lane < row, 0.0, body))
    rolled = pltpu.roll(body, HALF, 1)
    at = lane - HALF
    bottom = jnp.where(at == row, 0.5 * diagonal, jnp.where((at >= 0) & (at < row), rolled, 0.0))
    folded = jnp.concatenate([top, bottom], 0)
    return folded + turned(folded)


def fill(target, slot, face, packed):
    target[slot, pl.ds(0, SIDE), :] = face
    if packed is not None:
        target[slot, pl.ds(SIDE, HALF), :] = packed[0]
        target[slot, pl.ds(SIDE + HALF, PACKED - HALF), :] = packed[1]


def pack_kernel(own, to_right, to_left, to_partner):
    for slot in range(own.shape[0]):
        packed = pack(symmetric(own[slot, 0]))
        fill(to_right, slot, own[slot, 2], packed)
        fill(to_left, slot, own[slot, 1], packed)
        fill(to_partner, slot, own[slot, 3], packed)


def my_links(lists, cols, slots):
    my_row = lax.axis_index("row")
    device = my_row * cols + lax.axis_index("col")
    links = []
    for slot in range(slots):
        column = device * slots + slot
        present = [jnp.where(lists[column, k] >= 0, 1.0, 0.0).astype(f32) for k in range(4)]
        partner_row = lists[column, 3] // (slots * cols)
        links.append((present, jnp.bitwise_xor(my_row, partner_row)))
    return links


def neighbour_parts(slot, bit, received, with_diagonals):
    from_left, from_right = received[:2]
    from_rows = received[2:]

    def read(first, count):
        span = pl.ds(first, count)
        partner = from_rows[0][slot, span, :]
        for place in range(1, len(from_rows)):
            partner = jnp.where(bit == (1 << place), from_rows[place][slot, span, :], partner)
        return from_left[slot, span, :], from_right[slot, span, :], partner

    faces = read(0, SIDE)
    if not with_diagonals:
        return faces, None
    bodies = read(SIDE, HALF)
    diagonals = read(SIDE + HALF, PACKED - HALF)
    return faces, [unpack(b, d[0:1, :]) for b, d in zip(bodies, diagonals)]


def assemble_kernel(cols, members, has_base, *refs):
    lists, own = refs[:2]
    base = refs[2] if has_base else None
    received = refs[2 + has_base : -7]
    blocks, cube, norms, s_high, s_low, q_high, q_low = refs[-7:]
    slots = own.shape[0]
    order = members * SIDE
    top = None
    links = my_links(lists, cols, slots)
    for slot in range(slots):
        present, bit = links[slot]
        faces, diagonals = neighbour_parts(slot, bit, received, True)

        def place(row, col, value):
            high, low = split(value)
            at = (slot, pl.ds(row * SIDE, SIDE), pl.ds(col * SIDE, SIDE))
            s_high[at] = high
            s_low[at] = low

        centre = symmetric(own[slot, 0])
        if has_base:
            centre = centre + base[slot, 0]
        blocks[slot, 0] = centre
        place(0, 0, centre)
        empty = jnp.zeros((SIDE, SIDE), bf16)
        for k in range(1, members):
            column = present[k] * (0.5 * (own[slot, k] + turned(faces[k - 1])))
            block = present[k] * diagonals[k - 1]
            if has_base:
                column = column + base[slot, k]
                block = block + base[slot, members - 1 + k]
            blocks[slot, k] = column
            blocks[slot, members - 1 + k] = block
            place(k, 0, column)
            place(0, k, turned(column))
            place(k, k, block)
            for other in range(1, members):
                if other != k:
                    at = (slot, pl.ds(k * SIDE, SIDE), pl.ds(other * SIDE, SIDE))
                    s_high[at] = empty
                    s_low[at] = empty
    for slot in range(slots):
        matrix = (s_high.at[slot], s_low.at[slot])
        total = None
        for rows, columns, off in upper_tiles(order):
            tile = product(matrix, matrix, rows, columns)
            part = jnp.sum(tile * tile, axis=0, keepdims=True)
            part = 2.0 * part if off else part
            total = part if total is None else total + part
            high, low = split(tile)
            q_high[slot, rows, columns] = high
            q_low[slot, rows, columns] = low
            if off:
                high, low = split(turned(tile))
                q_high[slot, columns, rows] = high
                q_low[slot, columns, rows] = low
        total = jnp.sum(total, axis=1, keepdims=True)
        top = total if top is None else jnp.maximum(top, total)
    norms[...] = jnp.broadcast_to(top.reshape(1, 1, 1), norms.shape)
    for slot in range(slots):
        matrix = (s_high.at[slot], s_low.at[slot])
        square = (q_high.at[slot], q_low.at[slot])
        for rows, columns, off in upper_tiles(order):
            cube[slot, rows, columns] = product(matrix, square, rows, columns)


def sign_kernel(members, last, norms, blocks, cube, own, to_right, to_left, to_partner, x, xh, xl, yh, yl):
    slots = blocks.shape[0]
    order = members * SIDE
    largest = jnp.max(jnp.max(norms[...], axis=0), axis=(0, 1), keepdims=True)
    scaling = 1.5 / jnp.sqrt(jnp.sqrt(largest + epsilon))
    linear = 1.5 * scaling
    cubic = -0.5 * (scaling * scaling * scaling)

    def keep(now, slot, rows, columns, value, mirror):
        high, low = split(value)
        x[slot, rows, columns] = value
        xh[now, slot, rows, columns] = high
        xl[now, slot, rows, columns] = low
        if mirror:
            high, low = split(turned(value))
            xh[now, slot, columns, rows] = high
            xl[now, slot, columns, rows] = low

    for slot in range(slots):
        for i in range(members):
            for j in range(i, members):
                rows, columns = pl.ds(i * SIDE, SIDE), pl.ds(j * SIDE, SIDE)
                value = cubic * cube[slot, rows, columns]
                if i == 0 and j > 0:
                    value = value + linear * turned(blocks[slot, j])
                elif i == j:
                    value = value + linear * blocks[slot, members - 1 + i if i else 0]
                keep(0, slot, rows, columns, value, i != j)
                if i != j and i // 2 == j // 2:
                    x[slot, columns, rows] = turned(value)
    now = 0
    for repeat in range(1, ITERS - 1):
        for slot in range(slots):
            iterate = (xh.at[now, slot], xl.at[now, slot])
            for rows, columns, off in upper_tiles(order):
                tile = product(iterate, iterate, rows, columns)
                high, low = split(tile)
                yh[slot, rows, columns] = high
                yl[slot, rows, columns] = low
                if off:
                    high, low = split(turned(tile))
                    yh[slot, columns, rows] = high
                    yl[slot, columns, rows] = low
        for slot in range(slots):
            iterate = (xh.at[now, slot], xl.at[now, slot])
            square = (yh.at[slot], yl.at[slot])
            for rows, columns, off in upper_tiles(order):
                tile = product(iterate, square, rows, columns)
                value = 1.5 * x[slot, rows, columns] - 0.5 * tile
                keep(1 - now, slot, rows, columns, value, off)
                if off and repeat == ITERS - 2:
                    x[slot, columns, rows] = turned(value)
        now = 1 - now
    first = pl.ds(0, SIDE)

    def thin(slot, high, low):
        left_high, left_low = xh[now, slot], xl[now, slot]
        both = dot(left_high, jnp.concatenate([high, low], 1))
        return both[:, :SIDE] + both[:, SIDE:] + dot(left_low, high)

    middle = [thin(slot, xh[now, slot, :, first], xl[now, slot, :, first]) for slot in range(slots)]
    outer = [thin(slot, *split(middle[slot])) for slot in range(slots)]
    square = (SIDE, SIDE)
    eye = jnp.where(lanes(square) == rows_of(square), 0.5, 0.0)
    for slot in range(slots):
        central = 0.25 * outer[slot] - 0.75 * x[slot, :, first]
        parts = [central[k * SIDE : (k + 1) * SIDE] for k in range(members)]
        parts[0] = parts[0] + eye
        for k in range(members):
            own[slot, k] = parts[k]
        packed = None if last else pack(symmetric(parts[0]))
        fill(to_right, slot, parts[2], packed)
        fill(to_left, slot, parts[1], packed)
        fill(to_partner, slot, parts[3], packed)


def density_kernel(cols, members, *refs):
    lists, own = refs[:2]
    received = refs[2:-1]
    out = refs[-1]
    links = my_links(lists, cols, own.shape[0])
    for slot in range(own.shape[0]):
        present, bit = links[slot]
        faces, _ = neighbour_parts(slot, bit, received, False)
        out[slot, 0] = symmetric(own[slot, 0])
        for k in range(1, members):
            out[slot, k] = present[k] * (0.5 * (own[slot, k] + turned(faces[k - 1])))


def from_behind(block, axis, distance):
    devices = range(lax.axis_size(axis))
    return lax.ppermute(block, axis, [((i - distance) % len(devices), i) for i in devices])


def exchange(to_right, to_left, to_partner):
    received = [from_behind(to_right, "col", 1), from_behind(to_left, "col", -1)]
    rows = range(lax.axis_size("row"))
    place = 1
    while place < len(rows):
        received.append(lax.ppermute(to_partner, "row", [(i, i ^ place) for i in rows]))
        place *= 2
    return received


def vmem():
    return pl.BlockSpec(memory_space=pltpu.VMEM)


def smem():
    return pl.BlockSpec(memory_space=pltpu.SMEM)


def shape(*dims, dtype=f32):
    return jax.ShapeDtypeStruct(dims, dtype)


params = pltpu.CompilerParams(vmem_limit_bytes=48 * 1024 * 1024)


def per_device(hamiltonian, block_lists):
    slots, members = hamiltonian.shape[:2]
    order = members * SIDE
    cols = lax.axis_size("col")
    devices = lax.axis_size("row") * cols
    face = shape(slots, SIDE, SIDE)
    full = shape(slots, SIDE + PACKED, SIDE)

    sent = pl.pallas_call(
        pack_kernel,
        out_shape=[full] * 3,
        in_specs=[vmem()],
        out_specs=[vmem()] * 3,
        compiler_params=params,
        name="pack",
    )(hamiltonian)
    own = hamiltonian
    base = []
    for step in range(STEPS):
        last = step == STEPS - 1
        received = exchange(*sent)
        operands = [own, *base, *received]
        blocks, cube, norms = pl.pallas_call(
            functools.partial(assemble_kernel, cols, members, len(base)),
            out_shape=[
                shape(slots, 2 * members - 1, SIDE, SIDE),
                shape(slots, order, order),
                shape(devices, 8, SIDE),
            ],
            in_specs=[smem()] + [vmem()] * len(operands),
            out_specs=[vmem()] * 3,
            scratch_shapes=[pltpu.VMEM((slots, order, order), bf16)] * 4,
            compiler_params=params,
            name="assemble",
        )(block_lists, *operands)
        norms = lax.all_to_all(norms, ("row", "col"), 0, 0, tiled=True)
        own, *sent = pl.pallas_call(
            functools.partial(sign_kernel, members, last),
            out_shape=[shape(slots, members, SIDE, SIDE)] + [face if last else full] * 3,
            in_specs=[vmem()] * 3,
            out_specs=[vmem()] * 4,
            scratch_shapes=[pltpu.VMEM((slots, order, order), f32)]
            + [pltpu.VMEM((2, slots, order, order), bf16)] * 2
            + [pltpu.VMEM((slots, order, order), bf16)] * 2,
            compiler_params=params,
            name="sign",
        )(norms, blocks, cube)
        base = [blocks]
    received = exchange(*sent)
    return pl.pallas_call(
        functools.partial(density_kernel, cols, members),
        out_shape=shape(*hamiltonian.shape),
        in_specs=[smem()] + [vmem()] * (1 + len(received)),
        out_specs=vmem(),
        compiler_params=params,
        name="density",
    )(block_lists, own, *received)


def solution(mesh):
    return jax.shard_map(
        per_device,
        mesh=mesh,
        in_specs=(P(("row", "col"), None, None, None), P()),
        out_specs=P(("row", "col"), None, None, None),
        check_vma=False,
    )
```

```python
import functools
import jax
import jax.numpy as jnp
from jax import lax
from jax.experimental import pallas as pl
from jax.experimental.pallas import tpu as pltpu
from jax.sharding import PartitionSpec as P

ITERS = 6
STEPS = 2
SIDE = 128
HALF = SIDE // 2
PACKED = HALF + 8

epsilon = 1e-06
f32 = jnp.float32
bf16 = jnp.bfloat16


def turned(block):
    return jnp.swapaxes(block, -1, -2)


def symmetric(block):
    return 0.5 * (block + turned(block))


def split(values):
    high = values.astype(bf16)
    return high, (values - high.astype(f32)).astype(bf16)


def dot(left, right):
    return lax.dot_general(left, right, (((1,), (0,)), ((), ())), preferred_element_type=f32)


def product(left, right, rows, cols):
    left_high, left_low = left[0][rows, :], left[1][rows, :]
    right_high, right_low = right[0][:, cols], right[1][:, cols]
    return dot(
        jnp.concatenate([left_high, left_low, left_high], 1),
        jnp.concatenate([right_high, right_high, right_low], 0),
    )


def upper_tiles(order):
    tile = order // 2
    for place, (row, col) in enumerate(((0, 0), (0, 1), (1, 1))):
        yield place, pl.ds(row * tile, tile), pl.ds(col * tile, tile), row != col


def store_split(target, slot, rows, columns, value, mirror):
    high, low = split(value)
    target[0][slot, rows, columns] = high
    target[1][slot, rows, columns] = low
    if mirror:
        high, low = split(turned(value))
        target[0][slot, columns, rows] = high
        target[1][slot, columns, rows] = low


def lanes(shape):
    return lax.broadcasted_iota(jnp.int32, shape, 1)


def rows_of(shape):
    return lax.broadcasted_iota(jnp.int32, shape, 0)


def pack(block):
    shape = (HALF, SIDE)
    lower = pltpu.roll(block[HALF:, :], HALF, 1)
    body = jnp.where(lanes(shape) < rows_of(shape), lower, block[:HALF, :])
    whole = block.shape
    diagonal = jnp.sum(jnp.where(lanes(whole) == rows_of(whole), block, 0.0), 0, keepdims=True)
    return body, jnp.broadcast_to(diagonal, (PACKED - HALF, SIDE))


def unpack(body, diagonal):
    shape = (HALF, SIDE)
    lane, row = lanes(shape), rows_of(shape)
    top = jnp.where(lane == row, 0.5 * body, jnp.where(lane < row, 0.0, body))
    rolled = pltpu.roll(body, HALF, 1)
    at = lane - HALF
    bottom = jnp.where(at == row, 0.5 * diagonal, jnp.where((at >= 0) & (at < row), rolled, 0.0))
    folded = jnp.concatenate([top, bottom], 0)
    return folded + turned(folded)


def fill(target, slot, face, packed):
    target[slot, pl.ds(0, SIDE), :] = face
    if packed is not None:
        target[slot, pl.ds(SIDE, HALF), :] = packed[0]
        target[slot, pl.ds(SIDE + HALF, PACKED - HALF), :] = packed[1]


def pack_kernel(own, half, to_right, to_left, to_partner):
    for slot in range(own.shape[0]):
        centre = symmetric(own[slot, 0])
        packed = pack(centre)
        half[slot, 0] = centre
        for k in range(1, own.shape[1]):
            half[slot, k] = 0.5 * own[slot, k]
        fill(to_right, slot, own[slot, 2], packed)
        fill(to_left, slot, own[slot, 1], packed)
        fill(to_partner, slot, own[slot, 3], packed)


def my_links(lists, cols, slots):
    my_row = lax.axis_index("row")
    device = my_row * cols + lax.axis_index("col")
    links = []
    for slot in range(slots):
        column = device * slots + slot
        present = [jnp.where(lists[column, k] >= 0, 1.0, 0.0).astype(f32) for k in range(4)]
        partner_row = lists[column, 3] // (slots * cols)
        links.append((present, jnp.bitwise_xor(my_row, partner_row)))
    return links


def neighbour_parts(slot, bit, received, with_diagonals):
    from_left, from_right = received[:2]
    from_rows = received[2:]

    def read(first, count):
        span = pl.ds(first, count)
        partner = from_rows[0][slot, span, :]
        for place in range(1, len(from_rows)):
            partner = jnp.where(bit == (1 << place), from_rows[place][slot, span, :], partner)
        return from_left[slot, span, :], from_right[slot, span, :], partner

    faces = read(0, SIDE)
    if not with_diagonals:
        return faces, None
    bodies = read(SIDE, HALF)
    diagonals = read(SIDE + HALF, PACKED - HALF)
    return faces, [unpack(b, d[0:1, :]) for b, d in zip(bodies, diagonals)]


def assemble_kernel(cols, members, has_base, last, *refs):
    lists, half = refs[:2]
    base = refs[2] if has_base else None
    outputs = 6 + (not last)
    received = refs[2 + has_base : -outputs]
    norms, dense, s_high, s_low, q_high, q_low = refs[-outputs:][:6]
    blocks = None if last else refs[-1]
    slots = half.shape[0]
    order = members * SIDE
    top = None
    links = my_links(lists, cols, slots)
    for slot in range(slots):
        present, bit = links[slot]
        faces, diagonals = neighbour_parts(slot, bit, received, True)

        def place(row, col, value):
            high, low = split(value)
            at = (slot, pl.ds(row * SIDE, SIDE), pl.ds(col * SIDE, SIDE))
            s_high[at] = high
            s_low[at] = low
            if row // 2 <= col // 2:
                inner = (pl.ds(row % 2 * SIDE, SIDE), pl.ds(col % 2 * SIDE, SIDE))
                dense[(slot, row // 2 + col // 2, *inner)] = value

        centre = half[slot, 0]
        if has_base:
            centre = centre + base[slot, 0]
        if not last:
            blocks[slot, 0] = centre
        place(0, 0, centre)
        empty = jnp.zeros((SIDE, SIDE), f32)
        for k in range(1, members):
            column = present[k] * (half[slot, k] + 0.5 * turned(faces[k - 1]))
            block = present[k] * diagonals[k - 1]
            if has_base:
                column = column + base[slot, k]
                block = block + base[slot, members - 1 + k]
            if not last:
                blocks[slot, k] = column
                blocks[slot, members - 1 + k] = block
            place(k, 0, column)
            place(0, k, turned(column))
            place(k, k, block)
            for other in range(1, members):
                if other != k:
                    place(k, other, empty)
    for slot in range(slots):
        matrix = (s_high.at[slot], s_low.at[slot])
        total = None
        for _, rows, columns, off in upper_tiles(order):
            tile = product(matrix, matrix, rows, columns)
            part = jnp.sum(tile * tile, axis=0, keepdims=True)
            part = 2.0 * part if off else part
            total = part if total is None else total + part
            store_split((q_high, q_low), slot, rows, columns, tile, off)
        total = jnp.sum(total, axis=1, keepdims=True)
        top = total if top is None else jnp.maximum(top, total)
    norms[...] = jnp.broadcast_to(top.reshape(1, 1, 1), norms.shape)


def powers_kernel(s_high, s_low, q_high, q_low, powers, p_high, p_low):
    slots, count = powers.shape[:2]
    order = s_high.shape[1]
    for power in range(count):
        for slot in range(slots):
            square = (q_high.at[slot], q_low.at[slot])
            if power == 0:
                lower = (s_high.at[slot], s_low.at[slot])
            else:
                lower = (p_high.at[power % 2, slot], p_low.at[power % 2, slot])
            target = (p_high.at[1 - power % 2], p_low.at[1 - power % 2])
            for place, rows, columns, off in upper_tiles(order):
                tile = product(lower, square, rows, columns)
                powers[slot, power, place] = tile
                if power + 1 < count:
                    store_split(target, slot, rows, columns, tile, off)


def two_steps():
    once = {1: 1.5, 3: -0.5}
    cube = {0: 1.0}
    for _ in range(3):
        grown = {}
        for i, a in cube.items():
            for j, b in once.items():
                grown[i + j] = grown.get(i + j, 0.0) + a * b
        cube = grown
    return [1.5 * once.get(i, 0.0) - 0.5 * cube.get(i, 0.0) for i in range(1, 10, 2)]


def sign_kernel(members, last, norms, dense, powers, own, to_right, to_left, to_partner, x, xh, xl, yh, yl):
    slots = dense.shape[0]
    order = members * SIDE
    largest = jnp.max(jnp.max(norms[...], axis=0), axis=(0, 1), keepdims=True)
    scaling = 1.5 / jnp.sqrt(jnp.sqrt(largest + epsilon))
    factors, power = [], scaling
    for coefficient in two_steps():
        factors.append(coefficient * power)
        power = power * (scaling * scaling)
    for slot in range(slots):
        for place, rows, columns, off in upper_tiles(order):
            value = factors[0] * dense[slot, place]
            for k in range(1, len(factors)):
                value = value + factors[k] * powers[slot, k - 1, place]
            x[slot, rows, columns] = value
            store_split((xh.at[0], xl.at[0]), slot, rows, columns, value, off)
    now = 0
    for repeat in range(2, ITERS - 1):
        for slot in range(slots):
            iterate = (xh.at[now, slot], xl.at[now, slot])
            for _, rows, columns, off in upper_tiles(order):
                tile = product(iterate, iterate, rows, columns)
                store_split((yh, yl), slot, rows, columns, tile, off)
        for slot in range(slots):
            iterate = (xh.at[now, slot], xl.at[now, slot])
            square = (yh.at[slot], yl.at[slot])
            target = (xh.at[1 - now], xl.at[1 - now])
            for _, rows, columns, off in upper_tiles(order):
                tile = product(iterate, square, rows, columns)
                value = 1.5 * x[slot, rows, columns] - 0.5 * tile
                x[slot, rows, columns] = value
                store_split(target, slot, rows, columns, value, off)
                if off and repeat == ITERS - 2:
                    x[slot, columns, rows] = turned(value)
        now = 1 - now
    first = pl.ds(0, SIDE)

    def thin(slot, high, low):
        left_high, left_low = xh[now, slot], xl[now, slot]
        both = dot(left_high, jnp.concatenate([high, low], 1))
        return both[:, :SIDE] + both[:, SIDE:] + dot(left_low, high)

    middle = [thin(slot, xh[now, slot, :, first], xl[now, slot, :, first]) for slot in range(slots)]
    outer = [thin(slot, *split(middle[slot])) for slot in range(slots)]
    square = (SIDE, SIDE)
    eye = jnp.where(lanes(square) == rows_of(square), 0.5, 0.0)
    for slot in range(slots):
        central = 0.25 * outer[slot] - 0.75 * x[slot, :, first]
        parts = [central[k * SIDE : (k + 1) * SIDE] for k in range(members)]
        parts[0] = symmetric(parts[0]) + eye
        packed = None if last else pack(parts[0])
        fill(to_right, slot, parts[2], packed)
        fill(to_left, slot, parts[1], packed)
        fill(to_partner, slot, parts[3], packed)
        own[slot, 0] = parts[0]
        for k in range(1, members):
            own[slot, k] = 0.5 * parts[k]


def density_kernel(cols, members, *refs):
    lists, half = refs[:2]
    received = refs[2:-1]
    out = refs[-1]
    links = my_links(lists, cols, half.shape[0])
    for slot in range(half.shape[0]):
        present, bit = links[slot]
        faces, _ = neighbour_parts(slot, bit, received, False)
        out[slot, 0] = half[slot, 0]
        for k in range(1, members):
            out[slot, k] = present[k] * (half[slot, k] + 0.5 * turned(faces[k - 1]))


def from_behind(block, axis, distance):
    devices = range(lax.axis_size(axis))
    return lax.ppermute(block, axis, [((i - distance) % len(devices), i) for i in devices])


def exchange(to_right, to_left, to_partner):
    received = [from_behind(to_right, "col", 1), from_behind(to_left, "col", -1)]
    rows = range(lax.axis_size("row"))
    place = 1
    while place < len(rows):
        received.append(lax.ppermute(to_partner, "row", [(i, i ^ place) for i in rows]))
        place *= 2
    return received


def vmem():
    return pl.BlockSpec(memory_space=pltpu.VMEM)


def shape(*dims, dtype=f32):
    return jax.ShapeDtypeStruct(dims, dtype)


def call(kernel, name, operands, outputs, scratch=(), flops=0, smem_first=False):
    moved = sum(4 * a.size for a in (*operands, *outputs))
    specs = [vmem()] * len(operands)
    if smem_first:
        specs[0] = pl.BlockSpec(memory_space=pltpu.SMEM)
    return pl.pallas_call(
        kernel,
        out_shape=list(outputs),
        in_specs=specs,
        out_specs=[vmem()] * len(outputs),
        scratch_shapes=list(scratch),
        compiler_params=pltpu.CompilerParams(vmem_limit_bytes=24 * 1024 * 1024),
        cost_estimate=pl.CostEstimate(flops=flops, bytes_accessed=moved, transcendentals=0),
        name=name,
    )(*operands)


def per_device(hamiltonian, block_lists):
    slots, members = hamiltonian.shape[:2]
    order = members * SIDE
    tile = order // 2
    cols = lax.axis_size("col")
    devices = lax.axis_size("row") * cols
    face = shape(slots, SIDE, SIDE)
    full = shape(slots, SIDE + PACKED, SIDE)
    own = shape(slots, members, SIDE, SIDE)
    part = shape(slots, order, order, dtype=bf16)
    part_scratch = pltpu.VMEM((slots, order, order), bf16)
    both_scratch = pltpu.VMEM((2, slots, order, order), bf16)
    multiply = slots * 3 * 3 * order * order * order // 2
    count = len(two_steps()) - 1

    half, *sent = call(pack_kernel, "pack", [hamiltonian], [own] + [full] * 3)
    base = []
    for step in range(STEPS):
        last = step == STEPS - 1
        received = exchange(*sent)
        norms, dense, *parts = call(
            functools.partial(assemble_kernel, cols, members, len(base), last),
            "assemble",
            [block_lists, half, *base, *received],
            [shape(devices, 8, SIDE), shape(slots, 3, tile, tile)]
            + [part] * 4
            + ([] if last else [shape(slots, 2 * members - 1, SIDE, SIDE)]),
            flops=multiply,
            smem_first=True,
        )
        base = parts[4:]
        norms = lax.all_to_all(norms, ("row", "col"), 0, 0, tiled=True)
        (powers,) = call(
            powers_kernel,
            "powers",
            parts[:4],
            [shape(slots, count, 3, tile, tile)],
            [both_scratch] * 2,
            flops=count * multiply,
        )
        half, *sent = call(
            functools.partial(sign_kernel, members, last),
            "sign",
            [norms, dense, powers],
            [own] + [face if last else full] * 3,
            [pltpu.VMEM((slots, order, order), f32)] + [both_scratch] * 2 + [part_scratch] * 2,
            flops=7 * multiply,
        )
    received = exchange(*sent)
    (density,) = call(
        functools.partial(density_kernel, cols, members),
        "density",
        [block_lists, half, *received],
        [own],
        smem_first=True,
    )
    return density


def solution(mesh):
    return jax.shard_map(
        per_device,
        mesh=mesh,
        in_specs=(P(("row", "col"), None, None, None), P()),
        out_specs=P(("row", "col"), None, None, None),
        check_vma=False,
    )
```

```python
import functools
import jax
import jax.numpy as jnp
from jax import lax
from jax.experimental import pallas as pl
from jax.experimental.pallas import tpu as pltpu
from jax.sharding import PartitionSpec as P

ITERS = 6
STEPS = 2
SIDE = 128
HALF = SIDE // 2
PACKED = HALF + 8

epsilon = 1e-06
f32 = jnp.float32
bf16 = jnp.bfloat16


def turned(block):
    return jnp.swapaxes(block, -1, -2)


def symmetric(block):
    return 0.5 * (block + turned(block))


def split(values):
    high = values.astype(bf16)
    return high, (values - high.astype(f32)).astype(bf16)


def dot(left, right):
    return lax.dot_general(left, right, (((1,), (0,)), ((), ())), preferred_element_type=f32)


def product(left, right, rows, cols):
    left_high, left_low = left[0][rows, :], left[1][rows, :]
    right_high, right_low = right[0][:, cols], right[1][:, cols]
    return dot(
        jnp.concatenate([left_high, left_low, left_high], 1),
        jnp.concatenate([right_high, right_high, right_low], 0),
    )


def upper_tiles(order):
    tile = order // 2
    for place, (row, col) in enumerate(((0, 0), (0, 1), (1, 1))):
        yield place, pl.ds(row * tile, tile), pl.ds(col * tile, tile), row != col


def square_tiles(high, low, mixed):
    order = high.shape[0]
    first, second = pl.ds(0, order // 2), pl.ds(order // 2, order // 2)
    mixed[3] = dot(high[second, :], low[:, first])
    for place, rows, columns, off in upper_tiles(order):
        left = high[rows, :]
        mixed[place] = dot(left, low[:, columns])
        tile = dot(left, high[:, columns]) + (mixed[place] + turned(mixed[3 if off else place]))
        yield place, rows, columns, off, tile


def store_split(target, slot, rows, columns, value, mirror):
    high, low = split(value)
    target[0][slot, rows, columns] = high
    target[1][slot, rows, columns] = low
    if mirror:
        high, low = split(turned(value))
        target[0][slot, columns, rows] = high
        target[1][slot, columns, rows] = low


def store_arrow(target, slot, blocks):
    members = (len(blocks) + 1) // 2
    empty = jnp.zeros((SIDE, SIDE), f32)
    for row in range(members):
        for col in range(members):
            if col == 0:
                value = blocks[row]
            elif row == 0:
                value = turned(blocks[col])
            elif row == col:
                value = blocks[members - 1 + row]
            else:
                value = empty
            at = (pl.ds(row * SIDE, SIDE), pl.ds(col * SIDE, SIDE))
            store_split(target, slot, *at, value, False)


def lanes(shape):
    return lax.broadcasted_iota(jnp.int32, shape, 1)


def rows_of(shape):
    return lax.broadcasted_iota(jnp.int32, shape, 0)


TILE_BLOCKS = ((0, 1, None, 4), (2, 3, 5, 6), (7, 8, None, 9))


def pack(block):
    shape = (HALF, SIDE)
    lower = pltpu.roll(block[HALF:, :], HALF, 1)
    body = jnp.where(lanes(shape) < rows_of(shape), lower, block[:HALF, :])
    whole = block.shape
    diagonal = jnp.sum(jnp.where(lanes(whole) == rows_of(whole), block, 0.0), 0, keepdims=True)
    return body, jnp.broadcast_to(diagonal, (PACKED - HALF, SIDE))


def unpack(body, diagonal):
    shape = (HALF, SIDE)
    lane, row = lanes(shape), rows_of(shape)
    top = jnp.where(lane == row, 0.5 * body, jnp.where(lane < row, 0.0, body))
    rolled = pltpu.roll(body, HALF, 1)
    at = lane - HALF
    bottom = jnp.where(at == row, 0.5 * diagonal, jnp.where((at >= 0) & (at < row), rolled, 0.0))
    folded = jnp.concatenate([top, bottom], 0)
    return folded + turned(folded)


def fill(target, slot, face, packed):
    target[slot, pl.ds(0, SIDE), :] = face
    if packed is not None:
        target[slot, pl.ds(SIDE, HALF), :] = packed[0]
        target[slot, pl.ds(SIDE + HALF, PACKED - HALF), :] = packed[1]


def pack_kernel(own, half, to_right, to_left, to_partner):
    for slot in range(own.shape[0]):
        centre = symmetric(own[slot, 0])
        packed = pack(centre)
        half[slot, 0] = centre
        for k in range(1, own.shape[1]):
            half[slot, k] = 0.5 * own[slot, k]
        fill(to_right, slot, own[slot, 2], packed)
        fill(to_left, slot, own[slot, 1], packed)
        fill(to_partner, slot, own[slot, 3], packed)


def my_links(lists, cols, slots):
    my_row = lax.axis_index("row")
    device = my_row * cols + lax.axis_index("col")
    links = []
    for slot in range(slots):
        column = device * slots + slot
        present = [jnp.where(lists[column, k] >= 0, 1.0, 0.0).astype(f32) for k in range(4)]
        partner_row = lists[column, 3] // (slots * cols)
        links.append((present, jnp.bitwise_xor(my_row, partner_row)))
    return links


def neighbour_parts(slot, bit, received, with_diagonals):
    from_left, from_right = received[:2]
    from_rows = received[2:]

    def read(first, count):
        span = pl.ds(first, count)
        partner = from_rows[0][slot, span, :]
        for place in range(1, len(from_rows)):
            partner = jnp.where(bit == (1 << place), from_rows[place][slot, span, :], partner)
        return from_left[slot, span, :], from_right[slot, span, :], partner

    faces = read(0, SIDE)
    if not with_diagonals:
        return faces, None
    bodies = read(SIDE, HALF)
    diagonals = read(SIDE + HALF, PACKED - HALF)
    return faces, [unpack(b, d[0:1, :]) for b, d in zip(bodies, diagonals)]


def assemble_kernel(cols, members, has_base, *refs):
    lists, half = refs[:2]
    base = refs[2] if has_base else None
    received = refs[2 + has_base : -5]
    norms, blocks, s_high, s_low, mixed = refs[-5:]
    slots = half.shape[0]
    top = None
    links = my_links(lists, cols, slots)
    for slot in range(slots):
        present, bit = links[slot]
        faces, diagonals = neighbour_parts(slot, bit, received, True)
        parts = [half[slot, 0]]
        parts += [present[k] * (half[slot, k] + 0.5 * turned(faces[k - 1])) for k in range(1, members)]
        parts += [present[k] * diagonals[k - 1] for k in range(1, members)]
        if has_base:
            parts = [part + base[slot, place] for place, part in enumerate(parts)]
        for place, part in enumerate(parts):
            blocks[slot, place] = part
        store_arrow((s_high, s_low), slot, parts)
    for slot in range(slots):
        total = None
        for _, _, _, off, tile in square_tiles(s_high.at[slot], s_low.at[slot], mixed.at[slot]):
            part = jnp.sum(tile * tile, axis=0, keepdims=True)
            part = 2.0 * part if off else part
            total = part if total is None else total + part
        total = jnp.sum(total, axis=1, keepdims=True)
        top = total if top is None else jnp.maximum(top, total)
    norms[...] = jnp.broadcast_to(top.reshape(1, 1, 1), norms.shape)


def cube_kernel(blocks, out, s_high, s_low, q_high, q_low, mixed):
    slots, count = blocks.shape[:2]
    for slot in range(slots):
        parts = [blocks[slot, place] for place in range(count)]
        store_arrow((s_high, s_low), slot, parts)
        for place, part in enumerate(parts):
            out[slot, place] = part
    for slot in range(slots):
        for _, rows, columns, off, tile in square_tiles(s_high.at[slot], s_low.at[slot], mixed.at[slot]):
            store_split((q_high, q_low), slot, rows, columns, tile, off)
    for slot in range(slots):
        matrix = (s_high.at[slot], s_low.at[slot])
        square = (q_high.at[slot], q_low.at[slot])
        for place, rows, columns, _ in upper_tiles(s_high.shape[1]):
            tile = product(matrix, square, rows, columns)
            for inner, at in enumerate(TILE_BLOCKS[place]):
                if at is not None:
                    row, col = inner // 2 * SIDE, inner % 2 * SIDE
                    out[slot, count + at] = tile[row : row + SIDE, col : col + SIDE]


def sign_kernel(members, last, norms, source, own, to_right, to_left, to_partner, x, xh, xl, yh, yl, mixed):
    slots = source.shape[0]
    order = members * SIDE
    largest = jnp.max(jnp.max(norms[...], axis=0), axis=(0, 1), keepdims=True)
    scaling = 1.5 / jnp.sqrt(jnp.sqrt(largest + epsilon))
    linear = 1.5 * scaling
    cubic = -0.5 * (scaling * scaling * scaling)
    for slot in range(slots):
        at = 2 * members - 1
        for row in range(members):
            for col in range(row, members):
                value = cubic * source[slot, at]
                if row == col:
                    value = value + linear * source[slot, members - 1 + row if row else 0]
                elif row == 0:
                    value = value + linear * turned(source[slot, col])
                spans = (pl.ds(row * SIDE, SIDE), pl.ds(col * SIDE, SIDE))
                x[(slot, *spans)] = value
                if row // 2 == col // 2 and row != col:
                    x[(slot, *spans[::-1])] = turned(value)
                store_split((xh.at[0], xl.at[0]), slot, *spans, value, row != col)
                at += 1
    now = 0
    for repeat in range(1, ITERS - 1):
        for slot in range(slots):
            iterate = (xh.at[now, slot], xl.at[now, slot])
            for _, rows, columns, off, tile in square_tiles(*iterate, mixed.at[slot]):
                store_split((yh, yl), slot, rows, columns, tile, off)
        for slot in range(slots):
            iterate = (xh.at[now, slot], xl.at[now, slot])
            square = (yh.at[slot], yl.at[slot])
            target = (xh.at[1 - now], xl.at[1 - now])
            for _, rows, columns, off in upper_tiles(order):
                tile = product(iterate, square, rows, columns)
                value = 1.5 * x[slot, rows, columns] - 0.5 * tile
                x[slot, rows, columns] = value
                store_split(target, slot, rows, columns, value, off)
                if off and repeat == ITERS - 2:
                    x[slot, columns, rows] = turned(value)
        now = 1 - now
    first = pl.ds(0, SIDE)

    def thin(slot, high, low):
        left_high, left_low = xh[now, slot], xl[now, slot]
        both = dot(left_high, jnp.concatenate([high, low], 1))
        return both[:, :SIDE] + both[:, SIDE:] + dot(left_low, high)

    middle = [thin(slot, xh[now, slot, :, first], xl[now, slot, :, first]) for slot in range(slots)]
    outer = [thin(slot, *split(middle[slot])) for slot in range(slots)]
    square = (SIDE, SIDE)
    eye = jnp.where(lanes(square) == rows_of(square), 0.5, 0.0)
    for slot in range(slots):
        central = 0.25 * outer[slot] - 0.75 * x[slot, :, first]
        parts = [central[k * SIDE : (k + 1) * SIDE] for k in range(members)]
        parts[0] = symmetric(parts[0]) + eye
        packed = None if last else pack(parts[0])
        fill(to_right, slot, parts[2], packed)
        fill(to_left, slot, parts[1], packed)
        fill(to_partner, slot, parts[3], packed)
        own[slot, 0] = parts[0]
        for k in range(1, members):
            own[slot, k] = 0.5 * parts[k]


def density_kernel(cols, members, *refs):
    lists, half = refs[:2]
    received = refs[2:-1]
    out = refs[-1]
    links = my_links(lists, cols, half.shape[0])
    for slot in range(half.shape[0]):
        present, bit = links[slot]
        faces, _ = neighbour_parts(slot, bit, received, False)
        out[slot, 0] = half[slot, 0]
        for k in range(1, members):
            out[slot, k] = present[k] * (half[slot, k] + 0.5 * turned(faces[k - 1]))


def from_behind(block, axis, distance):
    devices = range(lax.axis_size(axis))
    return lax.ppermute(block, axis, [((i - distance) % len(devices), i) for i in devices])


def exchange(to_right, to_left, to_partner):
    received = [from_behind(to_right, "col", 1), from_behind(to_left, "col", -1)]
    rows = range(lax.axis_size("row"))
    place = 1
    while place < len(rows):
        received.append(lax.ppermute(to_partner, "row", [(i, i ^ place) for i in rows]))
        place *= 2
    return received


def vmem():
    return pl.BlockSpec(memory_space=pltpu.VMEM)


def shape(*dims, dtype=f32):
    return jax.ShapeDtypeStruct(dims, dtype)


def call(kernel, name, operands, outputs, scratch=(), flops=0, smem_first=False):
    moved = sum(4 * a.size for a in (*operands, *outputs))
    specs = [vmem()] * len(operands)
    if smem_first:
        specs[0] = pl.BlockSpec(memory_space=pltpu.SMEM)
    return pl.pallas_call(
        kernel,
        out_shape=list(outputs),
        in_specs=specs,
        out_specs=[vmem()] * len(outputs),
        scratch_shapes=list(scratch),
        compiler_params=pltpu.CompilerParams(vmem_limit_bytes=24 * 1024 * 1024),
        cost_estimate=pl.CostEstimate(flops=flops, bytes_accessed=moved, transcendentals=0),
        name=name,
    )(*operands)


def per_device(hamiltonian, block_lists):
    slots, members = hamiltonian.shape[:2]
    order = members * SIDE
    cols = lax.axis_size("col")
    devices = lax.axis_size("row") * cols
    face = shape(slots, SIDE, SIDE)
    full = shape(slots, SIDE + PACKED, SIDE)
    own = shape(slots, members, SIDE, SIDE)
    arrow = 2 * members - 1
    part_scratch = pltpu.VMEM((slots, order, order), bf16)
    both_scratch = pltpu.VMEM((2, slots, order, order), bf16)
    mixed_scratch = pltpu.VMEM((slots, 4, order // 2, order // 2), f32)
    multiply = slots * 3 * 3 * order * order * order // 2

    half, *sent = call(pack_kernel, "pack", [hamiltonian], [own] + [full] * 3)
    base = []
    for step in range(STEPS):
        last = step == STEPS - 1
        received = exchange(*sent)
        norms, blocks = call(
            functools.partial(assemble_kernel, cols, members, len(base)),
            "assemble",
            [block_lists, half, *base, *received],
            [shape(devices, 8, SIDE), shape(slots, arrow, SIDE, SIDE)],
            [part_scratch] * 2 + [mixed_scratch],
            flops=multiply,
            smem_first=True,
        )
        norms = lax.all_to_all(norms, ("row", "col"), 0, 0, tiled=True)
        (source,) = call(
            cube_kernel,
            "cube",
            [blocks],
            [shape(slots, arrow + members * (members + 1) // 2, SIDE, SIDE)],
            [part_scratch] * 4 + [mixed_scratch],
            flops=2 * multiply,
        )
        half, *sent = call(
            functools.partial(sign_kernel, members, last),
            "sign",
            [norms, source],
            [own] + [face if last else full] * 3,
            [pltpu.VMEM((slots, order, order), f32)] + [both_scratch] * 2 + [part_scratch] * 2 + [mixed_scratch],
            flops=8 * multiply,
        )
        base = [source]
    received = exchange(*sent)
    (density,) = call(
        functools.partial(density_kernel, cols, members),
        "density",
        [block_lists, half, *received],
        [own],
        smem_first=True,
    )
    return density


def solution(mesh):
    return jax.shard_map(
        per_device,
        mesh=mesh,
        in_specs=(P(("row", "col"), None, None, None), P()),
        out_specs=P(("row", "col"), None, None, None),
        check_vma=False,
    )
```

```python
import functools
import jax
import jax.numpy as jnp
from jax import lax
from jax.experimental import pallas as pl
from jax.experimental.pallas import tpu as pltpu
from jax.sharding import PartitionSpec as P

ITERS = 6
STEPS = 2
SIDE = 128
HALF = SIDE // 2
PACKED = HALF + 8

epsilon = 1e-06
f32 = jnp.float32
bf16 = jnp.bfloat16


def turned(block):
    return jnp.swapaxes(block, -1, -2)


def symmetric(block):
    return 0.5 * (block + turned(block))


def split(values):
    high = values.astype(bf16)
    return high, (values - high.astype(f32)).astype(bf16)


def dot(left, right):
    return lax.dot_general(left, right, (((1,), (0,)), ((), ())), preferred_element_type=f32)


def product(left, right, rows, cols):
    left_high, left_low = left[0][rows, :], left[1][rows, :]
    right_high, right_low = right[0][:, cols], right[1][:, cols]
    return dot(
        jnp.concatenate([left_high, left_low, left_high], 1),
        jnp.concatenate([right_high, right_high, right_low], 0),
    )


def upper_tiles(order):
    tile = order // 2
    for place, (row, col) in enumerate(((0, 0), (0, 1), (1, 1))):
        yield place, pl.ds(row * tile, tile), pl.ds(col * tile, tile), row != col


def square_tiles(high, low, mixed):
    order = high.shape[0]
    first, second = pl.ds(0, order // 2), pl.ds(order // 2, order // 2)
    mixed[3] = dot(high[second, :], low[:, first])
    for place, rows, columns, off in upper_tiles(order):
        left = high[rows, :]
        mixed[place] = dot(left, low[:, columns])
        tile = dot(left, high[:, columns]) + (mixed[place] + turned(mixed[3 if off else place]))
        yield place, rows, columns, off, tile


def store_split(target, slot, rows, columns, value, mirror):
    high, low = split(value)
    target[0][slot, rows, columns] = high
    target[1][slot, rows, columns] = low
    if mirror:
        high, low = split(turned(value))
        target[0][slot, columns, rows] = high
        target[1][slot, columns, rows] = low


def store_arrow(target, slot, blocks):
    members = (len(blocks) + 1) // 2
    empty = jnp.zeros((SIDE, SIDE), f32)
    for row in range(members):
        for col in range(members):
            if col == 0:
                value = blocks[row]
            elif row == 0:
                value = turned(blocks[col])
            elif row == col:
                value = blocks[members - 1 + row]
            else:
                value = empty
            at = (pl.ds(row * SIDE, SIDE), pl.ds(col * SIDE, SIDE))
            store_split(target, slot, *at, value, False)


def lanes(shape):
    return lax.broadcasted_iota(jnp.int32, shape, 1)


def rows_of(shape):
    return lax.broadcasted_iota(jnp.int32, shape, 0)


TILE_BLOCKS = ((0, 1, None, 4), (2, 3, 5, 6), (7, 8, None, 9))


def pack(block):
    shape = (HALF, SIDE)
    lower = pltpu.roll(block[HALF:, :], HALF, 1)
    body = jnp.where(lanes(shape) < rows_of(shape), lower, block[:HALF, :])
    whole = block.shape
    diagonal = jnp.sum(jnp.where(lanes(whole) == rows_of(whole), block, 0.0), 0, keepdims=True)
    return body, jnp.broadcast_to(diagonal, (PACKED - HALF, SIDE))


def unpack(body, diagonal):
    shape = (HALF, SIDE)
    lane, row = lanes(shape), rows_of(shape)
    top = jnp.where(lane == row, 0.5 * body, jnp.where(lane < row, 0.0, body))
    rolled = pltpu.roll(body, HALF, 1)
    at = lane - HALF
    bottom = jnp.where(at == row, 0.5 * diagonal, jnp.where((at >= 0) & (at < row), rolled, 0.0))
    folded = jnp.concatenate([top, bottom], 0)
    return folded + turned(folded)


def fill(target, slot, face, packed):
    target[slot, pl.ds(0, SIDE), :] = face
    if packed is not None:
        target[slot, pl.ds(SIDE, HALF), :] = packed[0]
        target[slot, pl.ds(SIDE + HALF, PACKED - HALF), :] = packed[1]


def fill_all(targets, slot, faces, packed):
    left, right, partner = faces
    even = lax.axis_index("col") % 2 == 0
    fill(targets[0], slot, jnp.where(even, right, left), packed)
    fill(targets[1], slot, jnp.where(even, left, right), packed)
    fill(targets[2], slot, partner, packed)


def pack_kernel(own, half, *targets):
    for slot in range(own.shape[0]):
        centre = symmetric(own[slot, 0])
        packed = pack(centre)
        half[slot, 0] = centre
        for k in range(1, own.shape[1]):
            half[slot, k] = 0.5 * own[slot, k]
        fill_all(targets, slot, [own[slot, k] for k in range(1, own.shape[1])], packed)


def links_kernel(slots, cols, lists, links):
    my_row = lax.axis_index("row")
    device = my_row * cols + lax.axis_index("col")
    count = links.shape[0] // slots
    for slot in range(slots):
        column = device * slots + slot
        partner_row = lists[column, 3] // (slots * cols)
        values = [jnp.where(lists[column, k] >= 0, 1.0, 0.0) for k in range(count - 1)]
        values.append(jnp.bitwise_xor(my_row, partner_row).astype(f32))
        for k, value in enumerate(values):
            links[pl.ds(slot * count + k, 1), :] = jnp.full((1, SIDE), value, f32)


def my_links(links, slots):
    count = links.shape[0] // slots
    rows = [links[pl.ds(place, 1), :] for place in range(slots * count)]
    return [(rows[slot * count : slot * count + count - 1], rows[slot * count + count - 1]) for slot in range(slots)]


def neighbour_parts(slot, bit, received, with_diagonals):
    from_even, from_odd = received[:2]
    from_rows = received[2:]
    even = lax.axis_index("col") % 2 == 0

    def read(first, count):
        span = pl.ds(first, count)
        partner = from_rows[0][slot, span, :]
        for place in range(1, len(from_rows)):
            partner = jnp.where(bit == float(1 << place), from_rows[place][slot, span, :], partner)
        near, far = from_even[slot, span, :], from_odd[slot, span, :]
        return jnp.where(even, far, near), jnp.where(even, near, far), partner

    faces = read(0, SIDE)
    if not with_diagonals:
        return faces, None
    bodies = read(SIDE, HALF)
    diagonals = read(SIDE + HALF, PACKED - HALF)
    return faces, [unpack(b, d[0:1, :]) for b, d in zip(bodies, diagonals)]


def assemble_kernel(members, has_base, *refs):
    links, half = refs[:2]
    base = refs[2] if has_base else None
    received = refs[2 + has_base : -5]
    norms, blocks, s_high, s_low, mixed = refs[-5:]
    slots = half.shape[0]
    top = None
    links = my_links(links, slots)
    for slot in range(slots):
        present, bit = links[slot]
        faces, diagonals = neighbour_parts(slot, bit, received, True)
        parts = [half[slot, 0]]
        parts += [present[k] * (half[slot, k] + 0.5 * turned(faces[k - 1])) for k in range(1, members)]
        parts += [present[k] * diagonals[k - 1] for k in range(1, members)]
        if has_base:
            parts = [part + base[slot, place] for place, part in enumerate(parts)]
        for place, part in enumerate(parts):
            blocks[slot, place] = part
        store_arrow((s_high, s_low), slot, parts)
    for slot in range(slots):
        total = None
        for _, _, _, off, tile in square_tiles(s_high.at[slot], s_low.at[slot], mixed.at[slot]):
            part = jnp.sum(tile * tile, axis=0, keepdims=True)
            part = 2.0 * part if off else part
            total = part if total is None else total + part
        total = jnp.sum(total, axis=1, keepdims=True)
        top = total if top is None else jnp.maximum(top, total)
    norms[...] = jnp.broadcast_to(top.reshape(1, 1, 1), norms.shape)


def cube_kernel(blocks, out, s_high, s_low, q_high, q_low, mixed):
    slots, count = blocks.shape[:2]
    for slot in range(slots):
        parts = [blocks[slot, place] for place in range(count)]
        store_arrow((s_high, s_low), slot, parts)
        for place, part in enumerate(parts):
            out[slot, place] = part
    for slot in range(slots):
        for _, rows, columns, off, tile in square_tiles(s_high.at[slot], s_low.at[slot], mixed.at[slot]):
            store_split((q_high, q_low), slot, rows, columns, tile, off)
    for slot in range(slots):
        matrix = (s_high.at[slot], s_low.at[slot])
        square = (q_high.at[slot], q_low.at[slot])
        for place, rows, columns, _ in upper_tiles(s_high.shape[1]):
            tile = product(matrix, square, rows, columns)
            for inner, at in enumerate(TILE_BLOCKS[place]):
                if at is not None:
                    row, col = inner // 2 * SIDE, inner % 2 * SIDE
                    out[slot, count + at] = tile[row : row + SIDE, col : col + SIDE]


def sign_kernel(members, last, norms, source, own, *refs):
    targets = refs[:3]
    x, xh, xl, yh, yl, mixed = refs[3:]
    slots = source.shape[0]
    order = members * SIDE
    largest = jnp.max(jnp.max(norms[...], axis=0), axis=(0, 1), keepdims=True)
    scaling = 1.5 / jnp.sqrt(jnp.sqrt(largest + epsilon))
    linear = 1.5 * scaling
    cubic = -0.5 * (scaling * scaling * scaling)
    for slot in range(slots):
        at = 2 * members - 1
        for row in range(members):
            for col in range(row, members):
                value = cubic * source[slot, at]
                if row == col:
                    value = value + linear * source[slot, members - 1 + row if row else 0]
                elif row == 0:
                    value = value + linear * turned(source[slot, col])
                spans = (pl.ds(row * SIDE, SIDE), pl.ds(col * SIDE, SIDE))
                x[(slot, *spans)] = value
                if row // 2 == col // 2 and row != col:
                    x[(slot, *spans[::-1])] = turned(value)
                store_split((xh.at[0], xl.at[0]), slot, *spans, value, row != col)
                at += 1
    now = 0
    for repeat in range(1, ITERS - 1):
        for slot in range(slots):
            iterate = (xh.at[now, slot], xl.at[now, slot])
            for _, rows, columns, off, tile in square_tiles(*iterate, mixed.at[slot]):
                store_split((yh, yl), slot, rows, columns, tile, off)
        for slot in range(slots):
            iterate = (xh.at[now, slot], xl.at[now, slot])
            square = (yh.at[slot], yl.at[slot])
            target = (xh.at[1 - now], xl.at[1 - now])
            for _, rows, columns, off in upper_tiles(order):
                tile = product(iterate, square, rows, columns)
                value = 1.5 * x[slot, rows, columns] - 0.5 * tile
                x[slot, rows, columns] = value
                store_split(target, slot, rows, columns, value, off)
                if off and repeat == ITERS - 2:
                    x[slot, columns, rows] = turned(value)
        now = 1 - now
    first = pl.ds(0, SIDE)

    def thin(slot, high, low):
        left_high, left_low = xh[now, slot], xl[now, slot]
        both = dot(left_high, jnp.concatenate([high, low], 1))
        return both[:, :SIDE] + both[:, SIDE:] + dot(left_low, high)

    middle = [thin(slot, xh[now, slot, :, first], xl[now, slot, :, first]) for slot in range(slots)]
    outer = [thin(slot, *split(middle[slot])) for slot in range(slots)]
    square = (SIDE, SIDE)
    eye = jnp.where(lanes(square) == rows_of(square), 0.5, 0.0)
    for slot in range(slots):
        central = 0.25 * outer[slot] - 0.75 * x[slot, :, first]
        parts = [central[k * SIDE : (k + 1) * SIDE] for k in range(members)]
        parts[0] = symmetric(parts[0]) + eye
        packed = None if last else pack(parts[0])
        fill_all(targets, slot, parts[1:], packed)
        own[slot, 0] = parts[0]
        for k in range(1, members):
            own[slot, k] = 0.5 * parts[k]


def density_kernel(members, *refs):
    links, half = refs[:2]
    received = refs[2:-1]
    out = refs[-1]
    links = my_links(links, half.shape[0])
    for slot in range(half.shape[0]):
        present, bit = links[slot]
        faces, _ = neighbour_parts(slot, bit, received, False)
        out[slot, 0] = half[slot, 0]
        for k in range(1, members):
            out[slot, k] = present[k] * (half[slot, k] + 0.5 * turned(faces[k - 1]))


def exchange(over_even, over_odd, to_partner):
    cols = range(lax.axis_size("col"))
    rows = range(lax.axis_size("row"))
    odd = [(i, (i + 1 if i % 2 else i - 1) % len(cols)) for i in cols]
    received = [lax.ppermute(over_even, "col", [(i, i ^ 1) for i in cols])]
    received.append(lax.ppermute(over_odd, "col", odd))
    place = 1
    while place < len(rows):
        received.append(lax.ppermute(to_partner, "row", [(i, i ^ place) for i in rows]))
        place *= 2
    return received


def vmem():
    return pl.BlockSpec(memory_space=pltpu.VMEM)


def shape(*dims, dtype=f32):
    return jax.ShapeDtypeStruct(dims, dtype)


def call(kernel, name, operands, outputs, scratch=(), flops=0, smem_first=False):
    moved = sum(4 * a.size for a in (*operands, *outputs))
    specs = [vmem()] * len(operands)
    if smem_first:
        specs[0] = pl.BlockSpec(memory_space=pltpu.SMEM)
    return pl.pallas_call(
        kernel,
        out_shape=list(outputs),
        in_specs=specs,
        out_specs=[vmem()] * len(outputs),
        scratch_shapes=list(scratch),
        compiler_params=pltpu.CompilerParams(vmem_limit_bytes=24 * 1024 * 1024),
        cost_estimate=pl.CostEstimate(flops=flops, bytes_accessed=moved, transcendentals=0),
        name=name,
    )(*operands)


def per_device(hamiltonian, block_lists):
    slots, members = hamiltonian.shape[:2]
    order = members * SIDE
    cols = lax.axis_size("col")
    devices = lax.axis_size("row") * cols
    face = shape(slots, SIDE, SIDE)
    full = shape(slots, SIDE + PACKED, SIDE)
    own = shape(slots, members, SIDE, SIDE)
    arrow = 2 * members - 1
    part_scratch = pltpu.VMEM((slots, order, order), bf16)
    both_scratch = pltpu.VMEM((2, slots, order, order), bf16)
    mixed_scratch = pltpu.VMEM((slots, 4, order // 2, order // 2), f32)
    multiply = slots * 3 * 3 * order * order * order // 2

    half, *sent = call(pack_kernel, "pack", [hamiltonian], [own] + [full] * 3)
    (links,) = call(
        functools.partial(links_kernel, slots, cols),
        "links",
        [block_lists],
        [shape(slots * (members + 1), SIDE)],
        smem_first=True,
    )
    base = []
    for step in range(STEPS):
        last = step == STEPS - 1
        received = exchange(*sent)
        norms, blocks = call(
            functools.partial(assemble_kernel, members, len(base)),
            "assemble",
            [links, half, *base, *received],
            [shape(devices, 1, SIDE), shape(slots, arrow, SIDE, SIDE)],
            [part_scratch] * 2 + [mixed_scratch],
            flops=multiply,
        )
        norms = lax.all_to_all(norms, ("row", "col"), 0, 0, tiled=True)
        (source,) = call(
            cube_kernel,
            "cube",
            [blocks],
            [shape(slots, arrow + members * (members + 1) // 2, SIDE, SIDE)],
            [part_scratch] * 4 + [mixed_scratch],
            flops=2 * multiply,
        )
        half, *sent = call(
            functools.partial(sign_kernel, members, last),
            "sign",
            [norms, source],
            [own] + [face if last else full] * 3,
            [pltpu.VMEM((slots, order, order), f32)] + [both_scratch] * 2 + [part_scratch] * 2 + [mixed_scratch],
            flops=8 * multiply,
        )
        base = [source]
    received = exchange(*sent)
    (density,) = call(
        functools.partial(density_kernel, members),
        "density",
        [links, half, *received],
        [own],
    )
    return density


def solution(mesh):
    return jax.shard_map(
        per_device,
        mesh=mesh,
        in_specs=(P(("row", "col"), None, None, None), P()),
        out_specs=P(("row", "col"), None, None, None),
        check_vma=False,
    )
```

```python
import functools
import jax
import jax.numpy as jnp
from jax import lax
from jax.experimental import pallas as pl
from jax.experimental.pallas import tpu as pltpu
from jax.sharding import PartitionSpec as P

ITERS = 6
STEPS = 2
SIDE = 128
HALF = SIDE // 2
PACKED = HALF + 8

epsilon = 1e-06
f32 = jnp.float32
bf16 = jnp.bfloat16


def turned(block):
    return jnp.swapaxes(block, -1, -2)


def symmetric(block):
    return 0.5 * (block + turned(block))


def split(values):
    high = values.astype(bf16)
    return high, (values - high.astype(f32)).astype(bf16)


def dot(left, right):
    return lax.dot_general(left, right, (((1,), (0,)), ((), ())), preferred_element_type=f32)


def product(left, right, rows, cols):
    left_high, left_low = left[0][rows, :], left[1][rows, :]
    right_high, right_low = right[0][:, cols], right[1][:, cols]
    return dot(
        jnp.concatenate([left_high, left_low, left_high], 1),
        jnp.concatenate([right_high, right_high, right_low], 0),
    )


def upper_tiles(order):
    tile = order // 2
    for place, (row, col) in enumerate(((0, 0), (0, 1), (1, 1))):
        yield place, pl.ds(row * tile, tile), pl.ds(col * tile, tile), row != col


def square_tiles(high, low, mixed):
    order = high.shape[0]
    first, second = pl.ds(0, order // 2), pl.ds(order // 2, order // 2)
    mixed[3] = dot(high[second, :], low[:, first])
    for place, rows, columns, off in upper_tiles(order):
        left = high[rows, :]
        mixed[place] = dot(left, low[:, columns])
        tile = dot(left, high[:, columns]) + (mixed[place] + turned(mixed[3 if off else place]))
        yield place, rows, columns, off, tile


def store_split(target, slot, rows, columns, value, mirror):
    high, low = split(value)
    target[0][slot, rows, columns] = high
    target[1][slot, rows, columns] = low
    if mirror:
        high, low = split(turned(value))
        target[0][slot, columns, rows] = high
        target[1][slot, columns, rows] = low


def store_arrow(target, slot, blocks):
    members = (len(blocks) + 1) // 2
    empty = jnp.zeros((SIDE, SIDE), f32)
    for row in range(members):
        for col in range(members):
            if col == 0:
                value = blocks[row]
            elif row == 0:
                value = turned(blocks[col])
            elif row == col:
                value = blocks[members - 1 + row]
            else:
                value = empty
            at = (pl.ds(row * SIDE, SIDE), pl.ds(col * SIDE, SIDE))
            store_split(target, slot, *at, value, False)


def lanes(shape):
    return lax.broadcasted_iota(jnp.int32, shape, 1)


def rows_of(shape):
    return lax.broadcasted_iota(jnp.int32, shape, 0)


TILE_BLOCKS = ((0, 1, None, 4), (2, 3, 5, 6), (7, 8, None, 9))


def pack(block):
    shape = (HALF, SIDE)
    lower = pltpu.roll(block[HALF:, :], HALF, 1)
    body = jnp.where(lanes(shape) < rows_of(shape), lower, block[:HALF, :])
    whole = block.shape
    diagonal = jnp.sum(jnp.where(lanes(whole) == rows_of(whole), block, 0.0), 0, keepdims=True)
    return body, jnp.broadcast_to(diagonal, (PACKED - HALF, SIDE))


def unpack(body, diagonal):
    shape = (HALF, SIDE)
    lane, row = lanes(shape), rows_of(shape)
    top = jnp.where(lane == row, 0.5 * body, jnp.where(lane < row, 0.0, body))
    rolled = pltpu.roll(body, HALF, 1)
    at = lane - HALF
    bottom = jnp.where(at == row, 0.5 * diagonal, jnp.where((at >= 0) & (at < row), rolled, 0.0))
    folded = jnp.concatenate([top, bottom], 0)
    return folded + turned(folded)


def fill(target, slot, face, packed):
    target[slot, pl.ds(0, SIDE), :] = face
    if packed is not None:
        target[slot, pl.ds(SIDE, HALF), :] = packed[0]
        target[slot, pl.ds(SIDE + HALF, PACKED - HALF), :] = packed[1]


def fill_all(targets, slot, faces, packed):
    left, right, partner = faces
    even = lax.axis_index("col") % 2 == 0
    fill(targets[0], slot, jnp.where(even, right, left), packed)
    fill(targets[1], slot, jnp.where(even, left, right), packed)
    fill(targets[2], slot, partner, packed)


def pack_kernel(own, half, *targets):
    for slot in range(own.shape[0]):
        centre = symmetric(own[slot, 0])
        packed = pack(centre)
        half[slot, 0] = centre
        for k in range(1, own.shape[1]):
            half[slot, k] = 0.5 * own[slot, k]
        fill_all(targets, slot, [own[slot, k] for k in range(1, own.shape[1])], packed)


def links_kernel(slots, cols, lists, links):
    my_row = lax.axis_index("row")
    device = my_row * cols + lax.axis_index("col")
    count = links.shape[0] // slots
    for slot in range(slots):
        column = device * slots + slot
        partner_row = lists[column, 3] // (slots * cols)
        values = [jnp.where(lists[column, k] >= 0, 1.0, 0.0) for k in range(count - 1)]
        values.append(jnp.bitwise_xor(my_row, partner_row).astype(f32))
        for k, value in enumerate(values):
            links[pl.ds(slot * count + k, 1), :] = jnp.full((1, SIDE), value, f32)


def my_links(links, slots):
    count = links.shape[0] // slots
    rows = [links[pl.ds(place, 1), :] for place in range(slots * count)]
    return [(rows[slot * count : slot * count + count - 1], rows[slot * count + count - 1]) for slot in range(slots)]


def neighbour_parts(slot, bit, received, with_diagonals):
    from_even, from_odd = received[:2]
    from_rows = received[2:]
    even = lax.axis_index("col") % 2 == 0

    def read(first, count):
        span = pl.ds(first, count)
        partner = from_rows[0][slot, span, :]
        for place in range(1, len(from_rows)):
            partner = jnp.where(bit == float(1 << place), from_rows[place][slot, span, :], partner)
        near, far = from_even[slot, span, :], from_odd[slot, span, :]
        return jnp.where(even, far, near), jnp.where(even, near, far), partner

    faces = read(0, SIDE)
    if not with_diagonals:
        return faces, None
    bodies = read(SIDE, HALF)
    diagonals = read(SIDE + HALF, PACKED - HALF)
    return faces, [unpack(b, d[0:1, :]) for b, d in zip(bodies, diagonals)]


def assemble_kernel(members, has_base, *refs):
    links, half = refs[:2]
    base = refs[2] if has_base else None
    received = refs[2 + has_base : -5]
    norms, blocks, s_high, s_low, mixed = refs[-5:]
    slots = half.shape[0]
    top = None
    links = my_links(links, slots)
    for slot in range(slots):
        present, bit = links[slot]
        faces, diagonals = neighbour_parts(slot, bit, received, True)
        parts = [half[slot, 0]]
        parts += [present[k] * (half[slot, k] + 0.5 * turned(faces[k - 1])) for k in range(1, members)]
        parts += [present[k] * diagonals[k - 1] for k in range(1, members)]
        if has_base:
            parts = [part + base[slot, place] for place, part in enumerate(parts)]
        for place, part in enumerate(parts):
            blocks[slot, place] = part
        store_arrow((s_high, s_low), slot, parts)
    for slot in range(slots):
        total = None
        for _, _, _, off, tile in square_tiles(s_high.at[slot], s_low.at[slot], mixed.at[slot]):
            part = jnp.sum(tile * tile, axis=0, keepdims=True)
            part = 2.0 * part if off else part
            total = part if total is None else total + part
        total = jnp.sum(total, axis=1, keepdims=True)
        top = total if top is None else jnp.maximum(top, total)
    norms[...] = jnp.broadcast_to(top.reshape(1, 1, 1), norms.shape)


def cube_kernel(blocks, out, s_high, s_low, q_high, q_low, mixed):
    slots, count = blocks.shape[:2]
    for slot in range(slots):
        parts = [blocks[slot, place] for place in range(count)]
        store_arrow((s_high, s_low), slot, parts)
        for place, part in enumerate(parts):
            out[slot, place] = part
    for slot in range(slots):
        for _, rows, columns, off, tile in square_tiles(s_high.at[slot], s_low.at[slot], mixed.at[slot]):
            store_split((q_high, q_low), slot, rows, columns, tile, off)
    for slot in range(slots):
        matrix = (s_high.at[slot], s_low.at[slot])
        square = (q_high.at[slot], q_low.at[slot])
        for place, rows, columns, _ in upper_tiles(s_high.shape[1]):
            tile = product(matrix, square, rows, columns)
            for inner, at in enumerate(TILE_BLOCKS[place]):
                if at is not None:
                    row, col = inner // 2 * SIDE, inner % 2 * SIDE
                    out[slot, count + at] = tile[row : row + SIDE, col : col + SIDE]


def schedule(square, advance, slots, repeats):
    for repeat in range(repeats):
        for work in (square, advance):
            for slot in range(slots):
                for _ in work(slot, repeat):
                    pass


def sign_kernel(members, last, norms, source, own, *refs):
    targets = refs[:3]
    x, xh, xl, yh, yl, mixed = refs[3:]
    slots = source.shape[0]
    order = members * SIDE
    largest = jnp.max(norms[...], axis=0)
    scaling = 1.5 / jnp.sqrt(jnp.sqrt(largest + epsilon))
    linear = 1.5 * scaling
    cubic = -0.5 * (scaling * scaling * scaling)
    for slot in range(slots):
        at = 2 * members - 1
        for row in range(members):
            for col in range(row, members):
                value = cubic * source[slot, at]
                if row == col:
                    value = value + linear * source[slot, members - 1 + row if row else 0]
                elif row == 0:
                    value = value + linear * turned(source[slot, col])
                spans = (pl.ds(row * SIDE, SIDE), pl.ds(col * SIDE, SIDE))
                x[(slot, *spans)] = value
                if row // 2 == col // 2 and row != col:
                    x[(slot, *spans[::-1])] = turned(value)
                store_split((xh.at[0], xl.at[0]), slot, *spans, value, row != col)
                at += 1
    def square(slot, repeat):
        iterate = (xh.at[repeat % 2, slot], xl.at[repeat % 2, slot])
        for _, rows, columns, off, tile in square_tiles(*iterate, mixed.at[slot]):
            store_split((yh, yl), slot, rows, columns, tile, off)
            yield

    def advance(slot, repeat):
        iterate = (xh.at[repeat % 2, slot], xl.at[repeat % 2, slot])
        target = (xh.at[1 - repeat % 2], xl.at[1 - repeat % 2])
        for _, rows, columns, off in upper_tiles(order):
            tile = product(iterate, (yh.at[slot], yl.at[slot]), rows, columns)
            value = 1.5 * x[slot, rows, columns] - 0.5 * tile
            x[slot, rows, columns] = value
            store_split(target, slot, rows, columns, value, off)
            yield

    schedule(square, advance, slots, ITERS - 2)
    now = (ITERS - 2) % 2
    first = pl.ds(0, SIDE)

    def thin(slot, high, low):
        both = dot(jnp.concatenate([high, low], 0), xh[now, slot])
        return both[:SIDE] + both[SIDE:] + dot(high, xl[now, slot])

    middle = [thin(slot, xh[now, slot, first, :], xl[now, slot, first, :]) for slot in range(slots)]
    outer = [thin(slot, *split(middle[slot])) for slot in range(slots)]
    square = (SIDE, SIDE)
    eye = jnp.where(lanes(square) == rows_of(square), 0.5, 0.0)
    for slot in range(slots):
        central = 0.25 * outer[slot] - 0.75 * x[slot, first, :]
        parts = [turned(central[:, k * SIDE : (k + 1) * SIDE]) for k in range(members)]
        parts[0] = symmetric(parts[0]) + eye
        fill_all(targets, slot, parts[1:], None if last else pack(parts[0]))
        own[slot, 0] = parts[0]
        for k in range(1, members):
            own[slot, k] = 0.5 * parts[k]


def density_kernel(members, *refs):
    links, half = refs[:2]
    received = refs[2:-1]
    out = refs[-1]
    links = my_links(links, half.shape[0])
    for slot in range(half.shape[0]):
        present, bit = links[slot]
        faces, _ = neighbour_parts(slot, bit, received, False)
        out[slot, 0] = half[slot, 0]
        for k in range(1, members):
            out[slot, k] = present[k] * (half[slot, k] + 0.5 * turned(faces[k - 1]))


def exchange(over_even, over_odd, to_partner):
    cols = range(lax.axis_size("col"))
    rows = range(lax.axis_size("row"))
    odd = [(i, (i + 1 if i % 2 else i - 1) % len(cols)) for i in cols]
    received = [lax.ppermute(over_even, "col", [(i, i ^ 1) for i in cols])]
    received.append(lax.ppermute(over_odd, "col", odd))
    place = 1
    while place < len(rows):
        received.append(lax.ppermute(to_partner, "row", [(i, i ^ place) for i in rows]))
        place *= 2
    return received


def vmem():
    return pl.BlockSpec(memory_space=pltpu.VMEM)


def shape(*dims, dtype=f32):
    return jax.ShapeDtypeStruct(dims, dtype)


def call(kernel, name, operands, outputs, scratch=(), flops=0, smem_first=False):
    moved = sum(4 * a.size for a in (*operands, *outputs))
    specs = [vmem()] * len(operands)
    if smem_first:
        specs[0] = pl.BlockSpec(memory_space=pltpu.SMEM)
    return pl.pallas_call(
        kernel,
        out_shape=list(outputs),
        in_specs=specs,
        out_specs=[vmem()] * len(outputs),
        scratch_shapes=list(scratch),
        compiler_params=pltpu.CompilerParams(vmem_limit_bytes=24 * 1024 * 1024),
        cost_estimate=pl.CostEstimate(flops=flops, bytes_accessed=moved, transcendentals=0),
        name=name,
    )(*operands)


def per_device(hamiltonian, block_lists):
    slots, members = hamiltonian.shape[:2]
    order = members * SIDE
    cols = lax.axis_size("col")
    devices = lax.axis_size("row") * cols
    face = shape(slots, SIDE, SIDE)
    full = shape(slots, SIDE + PACKED, SIDE)
    own = shape(slots, members, SIDE, SIDE)
    arrow = 2 * members - 1
    part_scratch = pltpu.VMEM((slots, order, order), bf16)
    both_scratch = pltpu.VMEM((2, slots, order, order), bf16)
    mixed_scratch = pltpu.VMEM((slots, 4, order // 2, order // 2), f32)
    multiply = slots * 3 * 3 * order * order * order // 2

    half, *sent = call(pack_kernel, "pack", [hamiltonian], [own] + [full] * 3)
    (links,) = call(
        functools.partial(links_kernel, slots, cols),
        "links",
        [block_lists],
        [shape(slots * (members + 1), SIDE)],
        smem_first=True,
    )
    base = []
    for step in range(STEPS):
        last = step == STEPS - 1
        received = exchange(*sent)
        norms, blocks = call(
            functools.partial(assemble_kernel, members, len(base)),
            "assemble",
            [links, half, *base, *received],
            [shape(devices, 1, SIDE), shape(slots, arrow, SIDE, SIDE)],
            [part_scratch] * 2 + [mixed_scratch],
            flops=multiply,
        )
        norms = lax.all_to_all(norms, ("row", "col"), 0, 0, tiled=True)
        (source,) = call(
            cube_kernel,
            "cube",
            [blocks],
            [shape(slots, arrow + members * (members + 1) // 2, SIDE, SIDE)],
            [part_scratch] * 4 + [mixed_scratch],
            flops=2 * multiply,
        )
        half, *sent = call(
            functools.partial(sign_kernel, members, last),
            "sign",
            [norms, source],
            [own] + [face if last else full] * 3,
            [pltpu.VMEM((slots, order, order), f32)] + [both_scratch] * 2 + [part_scratch] * 2 + [mixed_scratch],
            flops=8 * multiply,
        )
        base = [source]
    received = exchange(*sent)
    (density,) = call(
        functools.partial(density_kernel, members),
        "density",
        [links, half, *received],
        [own],
    )
    return density


def solution(mesh):
    return jax.shard_map(
        per_device,
        mesh=mesh,
        in_specs=(P(("row", "col"), None, None, None), P()),
        out_specs=P(("row", "col"), None, None, None),
        check_vma=False,
    )
```

```python
import functools
import jax
import jax.numpy as jnp
from jax import lax
from jax.experimental import pallas as pl
from jax.experimental.pallas import tpu as pltpu
from jax.sharding import PartitionSpec as P

ITERS = 6
STEPS = 2
SIDE = 128
HALF = SIDE // 2
PACKED = HALF + 8

epsilon = 1e-06
f32 = jnp.float32
bf16 = jnp.bfloat16


def turned(block):
    return jnp.swapaxes(block, -1, -2)


def symmetric(block):
    return 0.5 * (block + turned(block))


def split(values):
    high = values.astype(bf16)
    return high, (values - high.astype(f32)).astype(bf16)


def dot(left, right):
    return lax.dot_general(left, right, (((1,), (0,)), ((), ())), preferred_element_type=f32)


def product(left, right, rows, cols):
    left_high, left_low = left[0][rows, :], left[1][rows, :]
    right_high, right_low = right[0][:, cols], right[1][:, cols]
    return dot(
        jnp.concatenate([left_high, left_low, left_high], 1),
        jnp.concatenate([right_high, right_high, right_low], 0),
    )


def upper_tiles(order):
    tile = order // 2
    for place, (row, col) in enumerate(((0, 0), (0, 1), (1, 1))):
        yield place, pl.ds(row * tile, tile), pl.ds(col * tile, tile), row != col


def square_tiles(high, low, mixed):
    order = high.shape[0]
    first, second = pl.ds(0, order // 2), pl.ds(order // 2, order // 2)
    mixed[3] = dot(high[second, :], low[:, first])
    for place, rows, columns, off in upper_tiles(order):
        left = high[rows, :]
        mixed[place] = dot(left, low[:, columns])
        tile = dot(left, high[:, columns]) + (mixed[place] + turned(mixed[3 if off else place]))
        yield place, rows, columns, off, tile


def store_split(target, slot, rows, columns, value, mirror):
    high, low = split(value)
    target[0][slot, rows, columns] = high
    target[1][slot, rows, columns] = low
    if mirror:
        high, low = split(turned(value))
        target[0][slot, columns, rows] = high
        target[1][slot, columns, rows] = low


def symmetric_tile(tile):
    half = tile.shape[0] // 2
    beside = tile[:half, half:]
    upper = jnp.concatenate([symmetric(tile[:half, :half]), beside], 1)
    lower = jnp.concatenate([turned(beside), symmetric(tile[half:, half:])], 1)
    return jnp.concatenate([upper, lower], 0)


def store_arrow(target, slot, blocks):
    members = (len(blocks) + 1) // 2
    empty = jnp.zeros((SIDE, SIDE), f32)
    for row in range(members):
        for col in range(members):
            if col == 0:
                value = blocks[row]
            elif row == 0:
                value = turned(blocks[col])
            elif row == col:
                value = blocks[members - 1 + row]
            else:
                value = empty
            at = (pl.ds(row * SIDE, SIDE), pl.ds(col * SIDE, SIDE))
            store_split(target, slot, *at, value, False)


def lanes(shape):
    return lax.broadcasted_iota(jnp.int32, shape, 1)


def rows_of(shape):
    return lax.broadcasted_iota(jnp.int32, shape, 0)


TILE_BLOCKS = ((0, 1, None, 4), (2, 3, 5, 6), (7, 8, None, 9))


def pack(block):
    shape = (HALF, SIDE)
    lower = pltpu.roll(block[HALF:, :], HALF, 1)
    body = jnp.where(lanes(shape) < rows_of(shape), lower, block[:HALF, :])
    whole = block.shape
    diagonal = jnp.sum(jnp.where(lanes(whole) == rows_of(whole), block, 0.0), 0, keepdims=True)
    return body, jnp.broadcast_to(diagonal, (PACKED - HALF, SIDE))


def unpack(body, diagonal):
    shape = (HALF, SIDE)
    lane, row = lanes(shape), rows_of(shape)
    top = jnp.where(lane == row, 0.5 * body, jnp.where(lane < row, 0.0, body))
    rolled = pltpu.roll(body, HALF, 1)
    at = lane - HALF
    bottom = jnp.where(at == row, 0.5 * diagonal, jnp.where((at >= 0) & (at < row), rolled, 0.0))
    folded = jnp.concatenate([top, bottom], 0)
    return folded + turned(folded)


def fill(target, slot, face, packed):
    target[slot, pl.ds(0, SIDE), :] = face
    if packed is not None:
        target[slot, pl.ds(SIDE, HALF), :] = packed[0]
        target[slot, pl.ds(SIDE + HALF, PACKED - HALF), :] = packed[1]


def fill_all(targets, slot, faces, packed):
    left, right, partner = faces
    even = lax.axis_index("col") % 2 == 0
    fill(targets[0], slot, jnp.where(even, right, left), packed)
    fill(targets[1], slot, jnp.where(even, left, right), packed)
    fill(targets[2], slot, partner, packed)


def pack_kernel(own, half, *targets):
    for slot in range(own.shape[0]):
        centre = symmetric(own[slot, 0])
        packed = pack(centre)
        half[slot, 0] = centre
        for k in range(1, own.shape[1]):
            half[slot, k] = 0.5 * own[slot, k]
        fill_all(targets, slot, [own[slot, k] for k in range(1, own.shape[1])], packed)


def links_kernel(slots, cols, lists, links):
    my_row = lax.axis_index("row")
    device = my_row * cols + lax.axis_index("col")
    count = links.shape[0] // slots
    for slot in range(slots):
        column = device * slots + slot
        partner_row = lists[column, 3] // (slots * cols)
        values = [jnp.where(lists[column, k] >= 0, 1.0, 0.0) for k in range(count - 1)]
        values.append(jnp.bitwise_xor(my_row, partner_row).astype(f32))
        for k, value in enumerate(values):
            links[pl.ds(slot * count + k, 1), :] = jnp.full((1, SIDE), value, f32)


def my_links(links, slots):
    count = links.shape[0] // slots
    rows = [links[pl.ds(place, 1), :] for place in range(slots * count)]
    return [(rows[slot * count : slot * count + count - 1], rows[slot * count + count - 1]) for slot in range(slots)]


def neighbour_parts(slot, bit, received, with_diagonals):
    from_even, from_odd = received[:2]
    from_rows = received[2:]
    even = lax.axis_index("col") % 2 == 0

    def read(first, count):
        span = pl.ds(first, count)
        partner = from_rows[0][slot, span, :]
        for place in range(1, len(from_rows)):
            partner = jnp.where(bit == float(1 << place), from_rows[place][slot, span, :], partner)
        near, far = from_even[slot, span, :], from_odd[slot, span, :]
        return jnp.where(even, far, near), jnp.where(even, near, far), partner

    faces = read(0, SIDE)
    if not with_diagonals:
        return faces, None
    bodies = read(SIDE, HALF)
    diagonals = read(SIDE + HALF, PACKED - HALF)
    return faces, [unpack(b, d[0:1, :]) for b, d in zip(bodies, diagonals)]


def assemble_kernel(members, has_base, *refs):
    links, half = refs[:2]
    base = refs[2] if has_base else None
    received = refs[2 + has_base : -5]
    norms, blocks, s_high, s_low, mixed = refs[-5:]
    slots = half.shape[0]
    top = None
    links = my_links(links, slots)
    for slot in range(slots):
        present, bit = links[slot]
        faces, diagonals = neighbour_parts(slot, bit, received, True)
        parts = [half[slot, 0]]
        parts += [present[k] * (half[slot, k] + 0.5 * turned(faces[k - 1])) for k in range(1, members)]
        parts += [present[k] * diagonals[k - 1] for k in range(1, members)]
        if has_base:
            parts = [part + base[slot, place] for place, part in enumerate(parts)]
        for place, part in enumerate(parts):
            blocks[slot, place] = part
        store_arrow((s_high, s_low), slot, parts)
    for slot in range(slots):
        total = None
        for _, _, _, off, tile in square_tiles(s_high.at[slot], s_low.at[slot], mixed.at[slot]):
            part = jnp.sum(tile * tile, axis=0, keepdims=True)
            part = 2.0 * part if off else part
            total = part if total is None else total + part
        total = jnp.sum(total, axis=1, keepdims=True)
        top = total if top is None else jnp.maximum(top, total)
    norms[...] = jnp.broadcast_to(top.reshape(1, 1, 1), norms.shape)


def cube_kernel(blocks, out, s_high, s_low, q_high, q_low, mixed):
    slots, count = blocks.shape[:2]
    for slot in range(slots):
        parts = [blocks[slot, place] for place in range(count)]
        store_arrow((s_high, s_low), slot, parts)
        for place, part in enumerate(parts):
            out[slot, place] = part
    for slot in range(slots):
        for _, rows, columns, off, tile in square_tiles(s_high.at[slot], s_low.at[slot], mixed.at[slot]):
            store_split((q_high, q_low), slot, rows, columns, tile, off)
    for slot in range(slots):
        matrix = (s_high.at[slot], s_low.at[slot])
        square = (q_high.at[slot], q_low.at[slot])
        for place, rows, columns, _ in upper_tiles(s_high.shape[1]):
            tile = product(matrix, square, rows, columns)
            for inner, at in enumerate(TILE_BLOCKS[place]):
                if at is not None:
                    row, col = inner // 2 * SIDE, inner % 2 * SIDE
                    out[slot, count + at] = tile[row : row + SIDE, col : col + SIDE]


def schedule(square, advance, slots, repeats):
    for repeat in range(repeats):
        for work in (square, advance):
            for slot in range(slots):
                for _ in work(slot, repeat):
                    pass


def sign_kernel(members, last, norms, source, own, *refs):
    targets = refs[:3]
    x, xh, xl, yh, yl, mixed = refs[3:]
    slots = source.shape[0]
    order = members * SIDE
    largest = jnp.max(norms[...], axis=0)
    scaling = 1.5 / jnp.sqrt(jnp.sqrt(largest + epsilon))
    linear = 1.5 * scaling
    cubic = -0.5 * (scaling * scaling * scaling)
    for slot in range(slots):
        at = 2 * members - 1
        for row in range(members):
            for col in range(row, members):
                value = cubic * (symmetric(source[slot, at]) if row == col else source[slot, at])
                if row == col:
                    value = value + linear * source[slot, members - 1 + row if row else 0]
                elif row == 0:
                    value = value + linear * turned(source[slot, col])
                spans = (pl.ds(row * SIDE, SIDE), pl.ds(col * SIDE, SIDE))
                x[(slot, *spans)] = value
                if row // 2 == col // 2 and row != col:
                    x[(slot, *spans[::-1])] = turned(value)
                store_split((xh.at[0], xl.at[0]), slot, *spans, value, row != col)
                at += 1
    def square(slot, repeat):
        iterate = (xh.at[repeat % 2, slot], xl.at[repeat % 2, slot])
        for _, rows, columns, off, tile in square_tiles(*iterate, mixed.at[slot]):
            store_split((yh, yl), slot, rows, columns, tile, off)
            yield

    def advance(slot, repeat):
        iterate = (xh.at[repeat % 2, slot], xl.at[repeat % 2, slot])
        target = (xh.at[1 - repeat % 2], xl.at[1 - repeat % 2])
        for _, rows, columns, off in upper_tiles(order):
            tile = product(iterate, (yh.at[slot], yl.at[slot]), rows, columns)
            if not off:
                tile = symmetric_tile(tile)
            value = 1.5 * x[slot, rows, columns] - 0.5 * tile
            x[slot, rows, columns] = value
            store_split(target, slot, rows, columns, value, off)
            yield

    schedule(square, advance, slots, ITERS - 2)
    now = (ITERS - 2) % 2
    first = pl.ds(0, SIDE)

    def thin(slot, high, low):
        both = dot(jnp.concatenate([high, low], 0), xh[now, slot])
        return both[:SIDE] + both[SIDE:] + dot(high, xl[now, slot])

    middle = [thin(slot, xh[now, slot, first, :], xl[now, slot, first, :]) for slot in range(slots)]
    outer = [thin(slot, *split(middle[slot])) for slot in range(slots)]
    square = (SIDE, SIDE)
    eye = jnp.where(lanes(square) == rows_of(square), 0.5, 0.0)
    for slot in range(slots):
        central = 0.25 * outer[slot] - 0.75 * x[slot, first, :]
        parts = [turned(central[:, k * SIDE : (k + 1) * SIDE]) for k in range(members)]
        parts[0] = symmetric(parts[0]) + eye
        fill_all(targets, slot, parts[1:], None if last else pack(parts[0]))
        own[slot, 0] = parts[0]
        for k in range(1, members):
            own[slot, k] = 0.5 * parts[k]


def density_kernel(members, *refs):
    links, half = refs[:2]
    received = refs[2:-1]
    out = refs[-1]
    links = my_links(links, half.shape[0])
    for slot in range(half.shape[0]):
        present, bit = links[slot]
        faces, _ = neighbour_parts(slot, bit, received, False)
        out[slot, 0] = half[slot, 0]
        for k in range(1, members):
            out[slot, k] = present[k] * (half[slot, k] + 0.5 * turned(faces[k - 1]))


def exchange(over_even, over_odd, to_partner):
    cols = range(lax.axis_size("col"))
    rows = range(lax.axis_size("row"))
    odd = [(i, (i + 1 if i % 2 else i - 1) % len(cols)) for i in cols]
    received = [lax.ppermute(over_even, "col", [(i, i ^ 1) for i in cols])]
    received.append(lax.ppermute(over_odd, "col", odd))
    place = 1
    while place < len(rows):
        received.append(lax.ppermute(to_partner, "row", [(i, i ^ place) for i in rows]))
        place *= 2
    return received


def vmem():
    return pl.BlockSpec(memory_space=pltpu.VMEM)


def shape(*dims, dtype=f32):
    return jax.ShapeDtypeStruct(dims, dtype)


def call(kernel, name, operands, outputs, scratch=(), flops=0, smem_first=False):
    moved = sum(4 * a.size for a in (*operands, *outputs))
    specs = [vmem()] * len(operands)
    if smem_first:
        specs[0] = pl.BlockSpec(memory_space=pltpu.SMEM)
    return pl.pallas_call(
        kernel,
        out_shape=list(outputs),
        in_specs=specs,
        out_specs=[vmem()] * len(outputs),
        scratch_shapes=list(scratch),
        compiler_params=pltpu.CompilerParams(vmem_limit_bytes=24 * 1024 * 1024),
        cost_estimate=pl.CostEstimate(flops=flops, bytes_accessed=moved, transcendentals=0),
        name=name,
    )(*operands)


def per_device(hamiltonian, block_lists):
    slots, members = hamiltonian.shape[:2]
    order = members * SIDE
    cols = lax.axis_size("col")
    devices = lax.axis_size("row") * cols
    face = shape(slots, SIDE, SIDE)
    full = shape(slots, SIDE + PACKED, SIDE)
    own = shape(slots, members, SIDE, SIDE)
    arrow = 2 * members - 1
    part_scratch = pltpu.VMEM((slots, order, order), bf16)
    both_scratch = pltpu.VMEM((2, slots, order, order), bf16)
    mixed_scratch = pltpu.VMEM((slots, 4, order // 2, order // 2), f32)
    multiply = slots * 3 * 3 * order * order * order // 2

    half, *sent = call(pack_kernel, "pack", [hamiltonian], [own] + [full] * 3)
    (links,) = call(
        functools.partial(links_kernel, slots, cols),
        "links",
        [block_lists],
        [shape(slots * (members + 1), SIDE)],
        smem_first=True,
    )
    base = []
    for step in range(STEPS):
        last = step == STEPS - 1
        received = exchange(*sent)
        norms, blocks = call(
            functools.partial(assemble_kernel, members, len(base)),
            "assemble",
            [links, half, *base, *received],
            [shape(devices, 1, SIDE), shape(slots, arrow, SIDE, SIDE)],
            [part_scratch] * 2 + [mixed_scratch],
            flops=multiply,
        )
        norms = lax.all_to_all(norms, ("row", "col"), 0, 0, tiled=True)
        (source,) = call(
            cube_kernel,
            "cube",
            [blocks],
            [shape(slots, arrow + members * (members + 1) // 2, SIDE, SIDE)],
            [part_scratch] * 4 + [mixed_scratch],
            flops=2 * multiply,
        )
        half, *sent = call(
            functools.partial(sign_kernel, members, last),
            "sign",
            [norms, source],
            [own] + [face if last else full] * 3,
            [pltpu.VMEM((slots, order, order), f32)] + [both_scratch] * 2 + [part_scratch] * 2 + [mixed_scratch],
            flops=8 * multiply,
        )
        base = [source]
    received = exchange(*sent)
    (density,) = call(
        functools.partial(density_kernel, members),
        "density",
        [links, half, *received],
        [own],
    )
    return density


def solution(mesh):
    return jax.shard_map(
        per_device,
        mesh=mesh,
        in_specs=(P(("row", "col"), None, None, None), P()),
        out_specs=P(("row", "col"), None, None, None),
        check_vma=False,
    )
```

```python
import functools
import jax
import jax.numpy as jnp
from jax import lax
from jax.experimental import pallas as pl
from jax.experimental.pallas import tpu as pltpu
from jax.sharding import PartitionSpec as P

ITERS = 6
STEPS = 2
SIDE = 128
HALF = SIDE // 2
PACKED = HALF + 8

epsilon = 1e-06
f32 = jnp.float32
bf16 = jnp.bfloat16


def turned(block):
    return jnp.swapaxes(block, -1, -2)


def symmetric(block):
    return 0.5 * (block + turned(block))


def split(values):
    high = values.astype(bf16)
    return high, (values - high.astype(f32)).astype(bf16)


def dot(left, right):
    return lax.dot_general(left, right, (((1,), (0,)), ((), ())), preferred_element_type=f32)


def span(first, count=1):
    return pl.ds(first * SIDE, count * SIDE)


STRIPS = (((0,), (0, 1)), ((1, 3), (1, 2)), ((2,), (2, 0)), ((3,), (3, 0)))
PLACES = tuple((row, col) for rows, cols in STRIPS for row in rows for col in cols)


def block_rows(matrix, rows):
    return jnp.concatenate([matrix[span(row), :] for row in rows], 0)


def block_columns(matrix, cols):
    return jnp.concatenate([matrix[:, span(col)] for col in cols], 1)


def blocks_of(strip, rows, cols):
    for i, row in enumerate(rows):
        for j, col in enumerate(cols):
            yield row, col, strip[i * SIDE : (i + 1) * SIDE, j * SIDE : (j + 1) * SIDE]


def product_blocks(left, right):
    for rows, cols in STRIPS:
        high, low = block_rows(left[0], rows), block_rows(left[1], rows)
        right_high, right_low = block_columns(right[0], cols), block_columns(right[1], cols)
        both = dot(jnp.concatenate([high, low], 0), right_high)
        count = high.shape[0]
        yield from blocks_of(both[:count] + both[count:] + dot(high, right_low), rows, cols)


def square_blocks(high, low, mixed):
    for first in range(0, high.shape[0] // SIDE, 2):
        mixed[:, span(first, 2)] = dot(high[...], low[:, span(first, 2)])
    for rows, cols in STRIPS:
        strip = dot(block_rows(high, rows), block_columns(high, cols))
        for row, col, block in blocks_of(strip, rows, cols):
            yield row, col, block + (mixed[span(row), span(col)] + turned(mixed[span(col), span(row)]))


def store_split(target, slot, rows, columns, value, mirror):
    high, low = split(value)
    target[0][slot, rows, columns] = high
    target[1][slot, rows, columns] = low
    if mirror:
        high, low = split(turned(value))
        target[0][slot, columns, rows] = high
        target[1][slot, columns, rows] = low


def store_arrow(target, slot, blocks):
    members = (len(blocks) + 1) // 2
    empty = jnp.zeros((SIDE, SIDE), f32)
    for row in range(members):
        for col in range(members):
            if col == 0:
                value = blocks[row]
            elif row == 0:
                value = turned(blocks[col])
            elif row == col:
                value = blocks[members - 1 + row]
            else:
                value = empty
            at = (pl.ds(row * SIDE, SIDE), pl.ds(col * SIDE, SIDE))
            store_split(target, slot, *at, value, False)


def lanes(shape):
    return lax.broadcasted_iota(jnp.int32, shape, 1)


def rows_of(shape):
    return lax.broadcasted_iota(jnp.int32, shape, 0)


def pack(block):
    shape = (HALF, SIDE)
    lower = pltpu.roll(block[HALF:, :], HALF, 1)
    body = jnp.where(lanes(shape) < rows_of(shape), lower, block[:HALF, :])
    whole = block.shape
    diagonal = jnp.sum(jnp.where(lanes(whole) == rows_of(whole), block, 0.0), 0, keepdims=True)
    return body, jnp.broadcast_to(diagonal, (PACKED - HALF, SIDE))


def unpack(body, diagonal):
    shape = (HALF, SIDE)
    lane, row = lanes(shape), rows_of(shape)
    top = jnp.where(lane == row, 0.5 * body, jnp.where(lane < row, 0.0, body))
    rolled = pltpu.roll(body, HALF, 1)
    at = lane - HALF
    bottom = jnp.where(at == row, 0.5 * diagonal, jnp.where((at >= 0) & (at < row), rolled, 0.0))
    folded = jnp.concatenate([top, bottom], 0)
    return folded + turned(folded)


def fill(target, slot, face, packed):
    target[slot, pl.ds(0, SIDE), :] = face
    if packed is not None:
        target[slot, pl.ds(SIDE, HALF), :] = packed[0]
        target[slot, pl.ds(SIDE + HALF, PACKED - HALF), :] = packed[1]


def fill_all(targets, slot, faces, packed):
    left, right, partner = faces
    even = lax.axis_index("col") % 2 == 0
    fill(targets[0], slot, jnp.where(even, right, left), packed)
    fill(targets[1], slot, jnp.where(even, left, right), packed)
    fill(targets[2], slot, partner, packed)


def pack_kernel(own, half, *targets):
    for slot in range(own.shape[0]):
        centre = symmetric(own[slot, 0])
        packed = pack(centre)
        half[slot, 0] = centre
        for k in range(1, own.shape[1]):
            half[slot, k] = 0.5 * own[slot, k]
        fill_all(targets, slot, [own[slot, k] for k in range(1, own.shape[1])], packed)


def links_kernel(slots, cols, lists, links):
    my_row = lax.axis_index("row")
    device = my_row * cols + lax.axis_index("col")
    count = links.shape[0] // slots
    for slot in range(slots):
        column = device * slots + slot
        partner_row = lists[column, 3] // (slots * cols)
        values = [jnp.where(lists[column, k] >= 0, 1.0, 0.0) for k in range(count - 1)]
        values.append(jnp.bitwise_xor(my_row, partner_row).astype(f32))
        for k, value in enumerate(values):
            links[pl.ds(slot * count + k, 1), :] = jnp.full((1, SIDE), value, f32)


def my_links(links, slots):
    count = links.shape[0] // slots
    rows = [links[pl.ds(place, 1), :] for place in range(slots * count)]
    return [(rows[slot * count : slot * count + count - 1], rows[slot * count + count - 1]) for slot in range(slots)]


def neighbour_parts(slot, bit, received, with_diagonals):
    from_even, from_odd = received[:2]
    from_rows = received[2:]
    even = lax.axis_index("col") % 2 == 0

    def read(first, count):
        part = pl.ds(first, count)
        partner = from_rows[0][slot, part, :]
        for place in range(1, len(from_rows)):
            partner = jnp.where(bit == float(1 << place), from_rows[place][slot, part, :], partner)
        near, far = from_even[slot, part, :], from_odd[slot, part, :]
        return jnp.where(even, far, near), jnp.where(even, near, far), partner

    faces = read(0, SIDE)
    if not with_diagonals:
        return faces, None
    bodies = read(SIDE, HALF)
    diagonals = read(SIDE + HALF, PACKED - HALF)
    return faces, [unpack(b, d[0:1, :]) for b, d in zip(bodies, diagonals)]


def assemble_kernel(members, has_base, *refs):
    links, half = refs[:2]
    base = refs[2] if has_base else None
    received = refs[2 + has_base : -5]
    norms, blocks, s_high, s_low, mixed = refs[-5:]
    slots = half.shape[0]
    top = None
    links = my_links(links, slots)
    for slot in range(slots):
        present, bit = links[slot]
        faces, diagonals = neighbour_parts(slot, bit, received, True)
        parts = [half[slot, 0]]
        parts += [present[k] * (half[slot, k] + 0.5 * turned(faces[k - 1])) for k in range(1, members)]
        parts += [present[k] * diagonals[k - 1] for k in range(1, members)]
        if has_base:
            parts = [part + base[slot, place] for place, part in enumerate(parts)]
        for place, part in enumerate(parts):
            blocks[slot, place] = part
        store_arrow((s_high, s_low), slot, parts)
    for slot in range(slots):
        total = None
        for row, col, block in square_blocks(s_high.at[slot], s_low.at[slot], mixed.at[slot]):
            part = jnp.sum(block * block, axis=0, keepdims=True)
            part = part if row == col else 2.0 * part
            total = part if total is None else total + part
        total = jnp.sum(total, axis=1, keepdims=True)
        top = total if top is None else jnp.maximum(top, total)
    norms[...] = jnp.broadcast_to(top.reshape(1, 1, 1), norms.shape)


def cube_kernel(blocks, out, s_high, s_low, q_high, q_low, mixed):
    slots, count = blocks.shape[:2]
    for slot in range(slots):
        parts = [blocks[slot, place] for place in range(count)]
        store_arrow((s_high, s_low), slot, parts)
        for place, part in enumerate(parts):
            out[slot, place] = part
    for slot in range(slots):
        for row, col, block in square_blocks(s_high.at[slot], s_low.at[slot], mixed.at[slot]):
            store_split((q_high, q_low), slot, span(row), span(col), block, row != col)
    for slot in range(slots):
        matrix = (s_high.at[slot], s_low.at[slot])
        square = (q_high.at[slot], q_low.at[slot])
        for place, (_, _, block) in enumerate(product_blocks(matrix, square)):
            out[slot, count + place] = block


def schedule(square, advance, slots, repeats):
    for repeat in range(repeats):
        for work in (square, advance):
            for slot in range(slots):
                for _ in work(slot, repeat):
                    pass


def sign_kernel(members, last, norms, source, own, *refs):
    targets = refs[:3]
    x, xh, xl, yh, yl, mixed = refs[3:]
    slots = source.shape[0]
    order = members * SIDE
    largest = jnp.max(norms[...], axis=0)
    scaling = 1.5 / jnp.sqrt(jnp.sqrt(largest + epsilon))
    linear = 1.5 * scaling
    cubic = -0.5 * (scaling * scaling * scaling)
    for slot in range(slots):
        for place, (row, col) in enumerate(PLACES):
            value = source[slot, 2 * members - 1 + place]
            value = cubic * (symmetric(value) if row == col else value)
            if row == col:
                value = value + linear * source[slot, members - 1 + row if row else 0]
            elif col == 0:
                value = value + linear * source[slot, row]
            elif row == 0:
                value = value + linear * turned(source[slot, col])
            x[slot, span(row), span(col)] = value
            store_split((xh.at[0], xl.at[0]), slot, span(row), span(col), value, row != col)

    def square(slot, repeat):
        iterate = (xh.at[repeat % 2, slot], xl.at[repeat % 2, slot])
        for row, col, block in square_blocks(*iterate, mixed.at[slot]):
            store_split((yh, yl), slot, span(row), span(col), block, row != col)
            yield

    def advance(slot, repeat):
        iterate = (xh.at[repeat % 2, slot], xl.at[repeat % 2, slot])
        target = (xh.at[1 - repeat % 2], xl.at[1 - repeat % 2])
        for row, col, block in product_blocks(iterate, (yh.at[slot], yl.at[slot])):
            at = (slot, span(row), span(col))
            value = 1.5 * x[at] - 0.5 * (symmetric(block) if row == col else block)
            x[at] = value
            store_split(target, *at, value, row != col)
            yield

    schedule(square, advance, slots, ITERS - 2)
    now = (ITERS - 2) % 2
    first = pl.ds(0, SIDE)

    def thin(slot, high, low):
        both = dot(jnp.concatenate([high, low], 0), xh[now, slot])
        return both[:SIDE] + both[SIDE:] + dot(high, xl[now, slot])

    middle = [thin(slot, xh[now, slot, first, :], xl[now, slot, first, :]) for slot in range(slots)]
    outer = [thin(slot, *split(middle[slot])) for slot in range(slots)]
    square = (SIDE, SIDE)
    eye = jnp.where(lanes(square) == rows_of(square), 0.5, 0.0)
    for slot in range(slots):
        parts = []
        for k in range(members):
            stored = x[slot, first, span(k)] if (0, k) in PLACES else turned(x[slot, span(k), first])
            parts.append(turned(0.25 * outer[slot][:, k * SIDE : (k + 1) * SIDE] - 0.75 * stored))
        parts[0] = symmetric(parts[0]) + eye
        fill_all(targets, slot, parts[1:], None if last else pack(parts[0]))
        own[slot, 0] = parts[0]
        for k in range(1, members):
            own[slot, k] = 0.5 * parts[k]


def density_kernel(members, *refs):
    links, half = refs[:2]
    received = refs[2:-1]
    out = refs[-1]
    links = my_links(links, half.shape[0])
    for slot in range(half.shape[0]):
        present, bit = links[slot]
        faces, _ = neighbour_parts(slot, bit, received, False)
        out[slot, 0] = half[slot, 0]
        for k in range(1, members):
            out[slot, k] = present[k] * (half[slot, k] + 0.5 * turned(faces[k - 1]))


def exchange(over_even, over_odd, to_partner):
    cols = range(lax.axis_size("col"))
    rows = range(lax.axis_size("row"))
    odd = [(i, (i + 1 if i % 2 else i - 1) % len(cols)) for i in cols]
    received = [lax.ppermute(over_even, "col", [(i, i ^ 1) for i in cols])]
    received.append(lax.ppermute(over_odd, "col", odd))
    place = 1
    while place < len(rows):
        received.append(lax.ppermute(to_partner, "row", [(i, i ^ place) for i in rows]))
        place *= 2
    return received


def vmem():
    return pl.BlockSpec(memory_space=pltpu.VMEM)


def shape(*dims, dtype=f32):
    return jax.ShapeDtypeStruct(dims, dtype)


def call(kernel, name, operands, outputs, scratch=(), flops=0, smem_first=False):
    moved = sum(4 * a.size for a in (*operands, *outputs))
    specs = [vmem()] * len(operands)
    if smem_first:
        specs[0] = pl.BlockSpec(memory_space=pltpu.SMEM)
    return pl.pallas_call(
        kernel,
        out_shape=list(outputs),
        in_specs=specs,
        out_specs=[vmem()] * len(outputs),
        scratch_shapes=list(scratch),
        compiler_params=pltpu.CompilerParams(vmem_limit_bytes=24 * 1024 * 1024),
        cost_estimate=pl.CostEstimate(flops=flops, bytes_accessed=moved, transcendentals=0),
        name=name,
    )(*operands)


def per_device(hamiltonian, block_lists):
    slots, members = hamiltonian.shape[:2]
    order = members * SIDE
    cols = lax.axis_size("col")
    devices = lax.axis_size("row") * cols
    face = shape(slots, SIDE, SIDE)
    full = shape(slots, SIDE + PACKED, SIDE)
    own = shape(slots, members, SIDE, SIDE)
    arrow = 2 * members - 1
    part_scratch = pltpu.VMEM((slots, order, order), bf16)
    both_scratch = pltpu.VMEM((2, slots, order, order), bf16)
    mixed_scratch = pltpu.VMEM((slots, order, order), f32)
    multiply = slots * 3 * 3 * order * order * order // 2

    half, *sent = call(pack_kernel, "pack", [hamiltonian], [own] + [full] * 3)
    (links,) = call(
        functools.partial(links_kernel, slots, cols),
        "links",
        [block_lists],
        [shape(slots * (members + 1), SIDE)],
        smem_first=True,
    )
    base = []
    for step in range(STEPS):
        last = step == STEPS - 1
        received = exchange(*sent)
        norms, blocks = call(
            functools.partial(assemble_kernel, members, len(base)),
            "assemble",
            [links, half, *base, *received],
            [shape(devices, 1, SIDE), shape(slots, arrow, SIDE, SIDE)],
            [part_scratch] * 2 + [mixed_scratch],
            flops=multiply,
        )
        norms = lax.all_to_all(norms, ("row", "col"), 0, 0, tiled=True)
        (source,) = call(
            cube_kernel,
            "cube",
            [blocks],
            [shape(slots, arrow + len(PLACES), SIDE, SIDE)],
            [part_scratch] * 4 + [mixed_scratch],
            flops=2 * multiply,
        )
        half, *sent = call(
            functools.partial(sign_kernel, members, last),
            "sign",
            [norms, source],
            [own] + [face if last else full] * 3,
            [pltpu.VMEM((slots, order, order), f32)] + [both_scratch] * 2 + [part_scratch] * 2 + [mixed_scratch],
            flops=8 * multiply,
        )
        base = [source]
    received = exchange(*sent)
    (density,) = call(
        functools.partial(density_kernel, members),
        "density",
        [links, half, *received],
        [own],
    )
    return density


def solution(mesh):
    return jax.shard_map(
        per_device,
        mesh=mesh,
        in_specs=(P(("row", "col"), None, None, None), P()),
        out_specs=P(("row", "col"), None, None, None),
        check_vma=False,
    )
```

```python
import functools
import jax
import jax.numpy as jnp
from jax import lax
from jax.experimental import pallas as pl
from jax.experimental.pallas import tpu as pltpu
from jax.sharding import PartitionSpec as P

ITERS = 6
STEPS = 2
SIDE = 128
HALF = SIDE // 2
EXTRA = 8

epsilon = 1e-06
f32 = jnp.float32
bf16 = jnp.bfloat16


def turned(block):
    return jnp.swapaxes(block, -1, -2)


def symmetric(block):
    return 0.5 * (block + turned(block))


def split(values):
    high = values.astype(bf16)
    return high, (values - high.astype(f32)).astype(bf16)


def dot(left, right):
    return lax.dot_general(left, right, (((1,), (0,)), ((), ())), preferred_element_type=f32)


def span(first, count=1):
    return pl.ds(first * SIDE, count * SIDE)


STRIPS = (((0,), (0, 1)), ((1, 3), (1, 2)), ((2,), (2, 0)), ((3,), (3, 0)))
PLACES = tuple((row, col) for rows, cols in STRIPS for row in rows for col in cols)


def block_rows(matrix, rows):
    return jnp.concatenate([matrix[span(row), :] for row in rows], 0)


def block_columns(matrix, cols):
    return jnp.concatenate([matrix[:, span(col)] for col in cols], 1)


def blocks_of(strip, rows, cols):
    for i, row in enumerate(rows):
        for j, col in enumerate(cols):
            yield row, col, strip[i * SIDE : (i + 1) * SIDE, j * SIDE : (j + 1) * SIDE]


def product_blocks(left, right):
    for rows, cols in STRIPS:
        high, low = block_rows(left[0], rows), block_rows(left[1], rows)
        right_high, right_low = block_columns(right[0], cols), block_columns(right[1], cols)
        both = dot(jnp.concatenate([high, low], 0), right_high)
        count = high.shape[0]
        yield from blocks_of(both[:count] + both[count:] + dot(high, right_low), rows, cols)


def square_blocks(high, low, mixed):
    for first in range(0, high.shape[0] // SIDE, 2):
        mixed[:, span(first, 2)] = dot(high[...], low[:, span(first, 2)])
    for rows, cols in STRIPS:
        strip = dot(block_rows(high, rows), block_columns(high, cols))
        for row, col, block in blocks_of(strip, rows, cols):
            yield row, col, block + (mixed[span(row), span(col)] + turned(mixed[span(col), span(row)]))


def store_split(target, slot, rows, columns, value, mirror):
    high, low = split(value)
    target[0][slot, rows, columns] = high
    target[1][slot, rows, columns] = low
    if mirror:
        high, low = split(turned(value))
        target[0][slot, columns, rows] = high
        target[1][slot, columns, rows] = low


def store_arrow(target, slot, blocks):
    members = (len(blocks) + 1) // 2
    empty = jnp.zeros((SIDE, SIDE), f32)
    for row in range(members):
        for col in range(members):
            if col == 0:
                value = blocks[row]
            elif row == 0:
                value = turned(blocks[col])
            elif row == col:
                value = blocks[members - 1 + row]
            else:
                value = empty
            at = (pl.ds(row * SIDE, SIDE), pl.ds(col * SIDE, SIDE))
            store_split(target, slot, *at, value, False)


def lanes(shape):
    return lax.broadcasted_iota(jnp.int32, shape, 1)


def rows_of(shape):
    return lax.broadcasted_iota(jnp.int32, shape, 0)


def pack(block):
    shape = (HALF, SIDE)
    lower = pltpu.roll(block[HALF:, :], HALF, 1)
    body = jnp.where(lanes(shape) < rows_of(shape), lower, block[:HALF, :])
    whole = block.shape
    return body, jnp.sum(jnp.where(lanes(whole) == rows_of(whole), block, 0.0), 0, keepdims=True)


def unpack(body, diagonal):
    shape = (HALF, SIDE)
    lane, row = lanes(shape), rows_of(shape)
    top = jnp.where(lane == row, 0.5 * body, jnp.where(lane < row, 0.0, body))
    rolled = pltpu.roll(body, HALF, 1)
    at = lane - HALF
    bottom = jnp.where(at == row, 0.5 * diagonal, jnp.where((at >= 0) & (at < row), rolled, 0.0))
    folded = jnp.concatenate([top, bottom], 0)
    return folded + turned(folded)


def message_rows(slots, with_diagonals):
    return slots * (SIDE + HALF) + EXTRA if with_diagonals else slots * SIDE


def fill(target, slot, face, packed):
    first = slot * (SIDE if packed is None else SIDE + HALF)
    target[pl.ds(first, SIDE), :] = face
    if packed is not None:
        body, diagonal = packed
        last = target.shape[0] - EXTRA
        target[pl.ds(first + SIDE, HALF), :] = body
        if slot == 0:
            target[pl.ds(last, EXTRA), :] = jnp.broadcast_to(diagonal, (EXTRA, SIDE))
        else:
            target[pl.ds(last + slot, 1), :] = diagonal


def fill_all(targets, slot, faces, packed):
    left, right, partner = faces
    even = lax.axis_index("col") % 2 == 0
    fill(targets[0], slot, jnp.where(even, right, left), packed)
    fill(targets[1], slot, jnp.where(even, left, right), packed)
    fill(targets[2], slot, partner, packed)


def pack_kernel(own, half, *targets):
    for slot in range(own.shape[0]):
        centre = symmetric(own[slot, 0])
        packed = pack(centre)
        half[slot, 0] = centre
        for k in range(1, own.shape[1]):
            half[slot, k] = 0.5 * own[slot, k]
        fill_all(targets, slot, [own[slot, k] for k in range(1, own.shape[1])], packed)


def links_kernel(slots, cols, lists, links):
    my_row = lax.axis_index("row")
    device = my_row * cols + lax.axis_index("col")
    count = links.shape[0] // slots
    for slot in range(slots):
        column = device * slots + slot
        partner_row = lists[column, 3] // (slots * cols)
        values = [jnp.where(lists[column, k] >= 0, 1.0, 0.0) for k in range(count - 1)]
        values.append(jnp.bitwise_xor(my_row, partner_row).astype(f32))
        for k, value in enumerate(values):
            links[pl.ds(slot * count + k, 1), :] = jnp.full((1, SIDE), value, f32)


def my_links(links, slots):
    count = links.shape[0] // slots
    rows = [links[pl.ds(place, 1), :] for place in range(slots * count)]
    return [(rows[slot * count : slot * count + count - 1], rows[slot * count + count - 1]) for slot in range(slots)]


def neighbour_parts(slot, bit, received, with_diagonals):
    from_even, from_odd = received[:2]
    from_rows = received[2:]
    even = lax.axis_index("col") % 2 == 0

    def read(first, count):
        part = pl.ds(first, count)
        partner = from_rows[0][part, :]
        for place in range(1, len(from_rows)):
            partner = jnp.where(bit == float(1 << place), from_rows[place][part, :], partner)
        near, far = from_even[part, :], from_odd[part, :]
        return jnp.where(even, far, near), jnp.where(even, near, far), partner

    start = slot * (SIDE + HALF if with_diagonals else SIDE)
    faces = read(start, SIDE)
    if not with_diagonals:
        return faces, None
    bodies = read(start + SIDE, HALF)
    diagonals = read(from_even.shape[0] - EXTRA + slot, 1)
    return faces, [unpack(body, diagonal) for body, diagonal in zip(bodies, diagonals)]


def assemble_kernel(members, has_base, *refs):
    links, half = refs[:2]
    base = refs[2] if has_base else None
    received = refs[2 + has_base : -5]
    norms, blocks, s_high, s_low, mixed = refs[-5:]
    slots = half.shape[0]
    top = None
    links = my_links(links, slots)
    for slot in range(slots):
        present, bit = links[slot]
        faces, diagonals = neighbour_parts(slot, bit, received, True)
        parts = [half[slot, 0]]
        parts += [present[k] * (half[slot, k] + 0.5 * turned(faces[k - 1])) for k in range(1, members)]
        parts += [present[k] * diagonals[k - 1] for k in range(1, members)]
        if has_base:
            parts = [part + base[slot, place] for place, part in enumerate(parts)]
        for place, part in enumerate(parts):
            blocks[slot, place] = part
        store_arrow((s_high, s_low), slot, parts)
    for slot in range(slots):
        total = None
        for row, col, block in square_blocks(s_high.at[slot], s_low.at[slot], mixed.at[slot]):
            part = jnp.sum(block * block, axis=0, keepdims=True)
            part = part if row == col else 2.0 * part
            total = part if total is None else total + part
        total = jnp.sum(total, axis=1, keepdims=True)
        top = total if top is None else jnp.maximum(top, total)
    norms[...] = jnp.broadcast_to(top.reshape(1, 1, 1), norms.shape)


def cube_kernel(blocks, out, s_high, s_low, q_high, q_low, mixed):
    slots, count = blocks.shape[:2]
    for slot in range(slots):
        parts = [blocks[slot, place] for place in range(count)]
        store_arrow((s_high, s_low), slot, parts)
        for place, part in enumerate(parts):
            out[slot, place] = part
    for slot in range(slots):
        for row, col, block in square_blocks(s_high.at[slot], s_low.at[slot], mixed.at[slot]):
            store_split((q_high, q_low), slot, span(row), span(col), block, row != col)
    for slot in range(slots):
        matrix = (s_high.at[slot], s_low.at[slot])
        square = (q_high.at[slot], q_low.at[slot])
        for place, (_, _, block) in enumerate(product_blocks(matrix, square)):
            out[slot, count + place] = block


def schedule(square, advance, slots, repeats):
    for repeat in range(repeats):
        for work in (square, advance):
            for slot in range(slots):
                for _ in work(slot, repeat):
                    pass


def sign_kernel(members, last, norms, source, own, *refs):
    targets = refs[:3]
    x, xh, xl, yh, yl, mixed = refs[3:]
    slots = source.shape[0]
    order = members * SIDE
    largest = jnp.max(norms[...], axis=0)
    scaling = 1.5 / jnp.sqrt(jnp.sqrt(largest + epsilon))
    linear = 1.5 * scaling
    cubic = -0.5 * (scaling * scaling * scaling)
    for slot in range(slots):
        for place, (row, col) in enumerate(PLACES):
            value = source[slot, 2 * members - 1 + place]
            value = cubic * (symmetric(value) if row == col else value)
            if row == col:
                value = value + linear * source[slot, members - 1 + row if row else 0]
            elif col == 0:
                value = value + linear * source[slot, row]
            elif row == 0:
                value = value + linear * turned(source[slot, col])
            x[slot, span(row), span(col)] = value
            store_split((xh.at[0], xl.at[0]), slot, span(row), span(col), value, row != col)

    def square(slot, repeat):
        iterate = (xh.at[repeat % 2, slot], xl.at[repeat % 2, slot])
        for row, col, block in square_blocks(*iterate, mixed.at[slot]):
            store_split((yh, yl), slot, span(row), span(col), block, row != col)
            yield

    def advance(slot, repeat):
        iterate = (xh.at[repeat % 2, slot], xl.at[repeat % 2, slot])
        target = (xh.at[1 - repeat % 2], xl.at[1 - repeat % 2])
        for row, col, block in product_blocks(iterate, (yh.at[slot], yl.at[slot])):
            at = (slot, span(row), span(col))
            value = 1.5 * x[at] - 0.5 * (symmetric(block) if row == col else block)
            x[at] = value
            store_split(target, *at, value, row != col)
            yield

    schedule(square, advance, slots, ITERS - 2)
    now = (ITERS - 2) % 2
    first = pl.ds(0, SIDE)

    def thin(slot, high, low):
        both = dot(jnp.concatenate([high, low], 0), xh[now, slot])
        return both[:SIDE] + both[SIDE:] + dot(high, xl[now, slot])

    middle = [thin(slot, xh[now, slot, first, :], xl[now, slot, first, :]) for slot in range(slots)]
    outer = [thin(slot, *split(middle[slot])) for slot in range(slots)]
    square = (SIDE, SIDE)
    eye = jnp.where(lanes(square) == rows_of(square), 0.5, 0.0)
    for slot in range(slots):
        parts = []
        for k in range(members):
            stored = x[slot, first, span(k)] if (0, k) in PLACES else turned(x[slot, span(k), first])
            parts.append(turned(0.25 * outer[slot][:, k * SIDE : (k + 1) * SIDE] - 0.75 * stored))
        parts[0] = symmetric(parts[0]) + eye
        fill_all(targets, slot, parts[1:], None if last else pack(parts[0]))
        own[slot, 0] = parts[0]
        for k in range(1, members):
            own[slot, k] = 0.5 * parts[k]


def density_kernel(members, *refs):
    links, half = refs[:2]
    received = refs[2:-1]
    out = refs[-1]
    links = my_links(links, half.shape[0])
    for slot in range(half.shape[0]):
        present, bit = links[slot]
        faces, _ = neighbour_parts(slot, bit, received, False)
        out[slot, 0] = half[slot, 0]
        for k in range(1, members):
            out[slot, k] = present[k] * (half[slot, k] + 0.5 * turned(faces[k - 1]))


def exchange(over_even, over_odd, to_partner):
    cols = range(lax.axis_size("col"))
    rows = range(lax.axis_size("row"))
    odd = [(i, (i + 1 if i % 2 else i - 1) % len(cols)) for i in cols]
    received = [lax.ppermute(over_even, "col", [(i, i ^ 1) for i in cols])]
    received.append(lax.ppermute(over_odd, "col", odd))
    place = 1
    while place < len(rows):
        received.append(lax.ppermute(to_partner, "row", [(i, i ^ place) for i in rows]))
        place *= 2
    return received


def vmem():
    return pl.BlockSpec(memory_space=pltpu.VMEM)


def shape(*dims, dtype=f32):
    return jax.ShapeDtypeStruct(dims, dtype)


def call(kernel, name, operands, outputs, scratch=(), flops=0, smem_first=False):
    moved = sum(4 * a.size for a in (*operands, *outputs))
    specs = [vmem()] * len(operands)
    if smem_first:
        specs[0] = pl.BlockSpec(memory_space=pltpu.SMEM)
    return pl.pallas_call(
        kernel,
        out_shape=list(outputs),
        in_specs=specs,
        out_specs=[vmem()] * len(outputs),
        scratch_shapes=list(scratch),
        compiler_params=pltpu.CompilerParams(vmem_limit_bytes=24 * 1024 * 1024),
        cost_estimate=pl.CostEstimate(flops=flops, bytes_accessed=moved, transcendentals=0),
        name=name,
    )(*operands)


def per_device(hamiltonian, block_lists):
    slots, members = hamiltonian.shape[:2]
    order = members * SIDE
    cols = lax.axis_size("col")
    devices = lax.axis_size("row") * cols
    face = shape(message_rows(slots, False), SIDE)
    full = shape(message_rows(slots, True), SIDE)
    own = shape(slots, members, SIDE, SIDE)
    arrow = 2 * members - 1
    part_scratch = pltpu.VMEM((slots, order, order), bf16)
    both_scratch = pltpu.VMEM((2, slots, order, order), bf16)
    mixed_scratch = pltpu.VMEM((slots, order, order), f32)
    multiply = slots * 3 * 3 * order * order * order // 2

    half, *sent = call(pack_kernel, "pack", [hamiltonian], [own] + [full] * 3)
    (links,) = call(
        functools.partial(links_kernel, slots, cols),
        "links",
        [block_lists],
        [shape(slots * (members + 1), SIDE)],
        smem_first=True,
    )
    base = []
    for step in range(STEPS):
        last = step == STEPS - 1
        received = exchange(*sent)
        norms, blocks = call(
            functools.partial(assemble_kernel, members, len(base)),
            "assemble",
            [links, half, *base, *received],
            [shape(devices, 1, SIDE), shape(slots, arrow, SIDE, SIDE)],
            [part_scratch] * 2 + [mixed_scratch],
            flops=multiply,
        )
        norms = lax.all_to_all(norms, ("row", "col"), 0, 0, tiled=True)
        (source,) = call(
            cube_kernel,
            "cube",
            [blocks],
            [shape(slots, arrow + len(PLACES), SIDE, SIDE)],
            [part_scratch] * 4 + [mixed_scratch],
            flops=2 * multiply,
        )
        half, *sent = call(
            functools.partial(sign_kernel, members, last),
            "sign",
            [norms, source],
            [own] + [face if last else full] * 3,
            [pltpu.VMEM((slots, order, order), f32)] + [both_scratch] * 2 + [part_scratch] * 2 + [mixed_scratch],
            flops=8 * multiply,
        )
        base = [source]
    received = exchange(*sent)
    (density,) = call(
        functools.partial(density_kernel, members),
        "density",
        [links, half, *received],
        [own],
    )
    return density


def solution(mesh):
    return jax.shard_map(
        per_device,
        mesh=mesh,
        in_specs=(P(("row", "col"), None, None, None), P()),
        out_specs=P(("row", "col"), None, None, None),
        check_vma=False,
    )
```

```python
import functools
import jax
import jax.numpy as jnp
from jax import lax
from jax.experimental import pallas as pl
from jax.experimental.pallas import tpu as pltpu
from jax.sharding import PartitionSpec as P

ITERS = 6
STEPS = 2
SIDE = 128
HALF = SIDE // 2
EXTRA = 8

epsilon = 1e-06
f32 = jnp.float32
bf16 = jnp.bfloat16


def turned(block):
    return jnp.swapaxes(block, -1, -2)


def symmetric(block):
    return 0.5 * (block + turned(block))


def split(values):
    high = values.astype(bf16)
    return high, (values - high.astype(f32)).astype(bf16)


def dot(left, right):
    return lax.dot_general(left, right, (((1,), (0,)), ((), ())), preferred_element_type=f32)


def span(first, count=1):
    return pl.ds(first * SIDE, count * SIDE)


STRIPS = (((0,), (0, 1)), ((1, 3), (1, 2)), ((2,), (2, 0)), ((3,), (3, 0)))
PLACES = tuple((row, col) for rows, cols in STRIPS for row in rows for col in cols)


def block_rows(matrix, rows):
    return jnp.concatenate([matrix[span(row), :] for row in rows], 0)


def block_columns(matrix, cols):
    return jnp.concatenate([matrix[:, span(col)] for col in cols], 1)


def blocks_of(strip, rows, cols):
    for i, row in enumerate(rows):
        for j, col in enumerate(cols):
            yield row, col, strip[i * SIDE : (i + 1) * SIDE, j * SIDE : (j + 1) * SIDE]


def product_blocks(left, right):
    for rows, cols in STRIPS:
        high, low = block_rows(left[0], rows), block_rows(left[1], rows)
        right_high, right_low = block_columns(right[0], cols), block_columns(right[1], cols)
        both = dot(jnp.concatenate([high, low], 0), right_high)
        count = high.shape[0]
        yield from blocks_of(both[:count] + both[count:] + dot(high, right_low), rows, cols)


def square_blocks(high, low, mixed):
    mixed[...] = dot(high[...], low[...])
    for rows, cols in STRIPS:
        strip = dot(block_rows(high, rows), block_columns(high, cols))
        for row, col, block in blocks_of(strip, rows, cols):
            yield row, col, block + (mixed[span(row), span(col)] + turned(mixed[span(col), span(row)]))


def store_split(target, slot, rows, columns, value, mirror):
    high, low = split(value)
    target[0][slot, rows, columns] = high
    target[1][slot, rows, columns] = low
    if mirror:
        high, low = split(turned(value))
        target[0][slot, columns, rows] = high
        target[1][slot, columns, rows] = low


def store_arrow(target, slot, blocks):
    members = (len(blocks) + 1) // 2
    empty = jnp.zeros((SIDE, SIDE), f32)
    for row in range(members):
        for col in range(members):
            if col == 0:
                value = blocks[row]
            elif row == 0:
                value = turned(blocks[col])
            elif row == col:
                value = blocks[members - 1 + row]
            else:
                value = empty
            at = (pl.ds(row * SIDE, SIDE), pl.ds(col * SIDE, SIDE))
            store_split(target, slot, *at, value, False)


def lanes(shape):
    return lax.broadcasted_iota(jnp.int32, shape, 1)


def rows_of(shape):
    return lax.broadcasted_iota(jnp.int32, shape, 0)


def pack(block):
    shape = (HALF, SIDE)
    lower = pltpu.roll(block[HALF:, :], HALF, 1)
    body = jnp.where(lanes(shape) < rows_of(shape), lower, block[:HALF, :])
    whole = block.shape
    return body, jnp.sum(jnp.where(lanes(whole) == rows_of(whole), block, 0.0), 0, keepdims=True)


def unpack(body, diagonal):
    shape = (HALF, SIDE)
    lane, row = lanes(shape), rows_of(shape)
    top = jnp.where(lane == row, 0.5 * body, jnp.where(lane < row, 0.0, body))
    rolled = pltpu.roll(body, HALF, 1)
    at = lane - HALF
    bottom = jnp.where(at == row, 0.5 * diagonal, jnp.where((at >= 0) & (at < row), rolled, 0.0))
    folded = jnp.concatenate([top, bottom], 0)
    return folded + turned(folded)


def message_rows(slots, with_diagonals):
    return slots * (SIDE + HALF) + EXTRA if with_diagonals else slots * SIDE


def fill(target, slot, face, packed):
    first = slot * (SIDE if packed is None else SIDE + HALF)
    target[pl.ds(first, SIDE), :] = face
    if packed is not None:
        body, diagonal = packed
        last = target.shape[0] - EXTRA
        target[pl.ds(first + SIDE, HALF), :] = body
        if slot == 0:
            target[pl.ds(last, EXTRA), :] = jnp.broadcast_to(diagonal, (EXTRA, SIDE))
        else:
            target[pl.ds(last + slot, 1), :] = diagonal


def fill_all(targets, slot, faces, packed):
    left, right, partner = faces
    even = lax.axis_index("col") % 2 == 0
    fill(targets[0], slot, jnp.where(even, right, left), packed)
    fill(targets[1], slot, jnp.where(even, left, right), packed)
    fill(targets[2], slot, partner, packed)


def pack_kernel(own, half, *targets):
    for slot in range(own.shape[0]):
        centre = symmetric(own[slot, 0])
        packed = pack(centre)
        half[slot, 0] = centre
        for k in range(1, own.shape[1]):
            half[slot, k] = 0.5 * own[slot, k]
        fill_all(targets, slot, [own[slot, k] for k in range(1, own.shape[1])], packed)


def links_kernel(slots, cols, lists, links):
    my_row = lax.axis_index("row")
    device = my_row * cols + lax.axis_index("col")
    count = links.shape[0] // slots
    for slot in range(slots):
        column = device * slots + slot
        partner_row = lists[column, 3] // (slots * cols)
        values = [jnp.where(lists[column, k] >= 0, 1.0, 0.0) for k in range(count - 1)]
        values.append(jnp.bitwise_xor(my_row, partner_row).astype(f32))
        for k, value in enumerate(values):
            links[pl.ds(slot * count + k, 1), :] = jnp.full((1, SIDE), value, f32)


def my_links(links, slots):
    count = links.shape[0] // slots
    rows = [links[pl.ds(place, 1), :] for place in range(slots * count)]
    return [(rows[slot * count : slot * count + count - 1], rows[slot * count + count - 1]) for slot in range(slots)]


def neighbour_parts(slot, bit, received, with_diagonals):
    from_even, from_odd = received[:2]
    from_rows = received[2:]
    even = lax.axis_index("col") % 2 == 0

    def read(first, count):
        part = pl.ds(first, count)
        partner = from_rows[0][part, :]
        for place in range(1, len(from_rows)):
            partner = jnp.where(bit == float(1 << place), from_rows[place][part, :], partner)
        near, far = from_even[part, :], from_odd[part, :]
        return jnp.where(even, far, near), jnp.where(even, near, far), partner

    start = slot * (SIDE + HALF if with_diagonals else SIDE)
    faces = read(start, SIDE)
    if not with_diagonals:
        return faces, None
    bodies = read(start + SIDE, HALF)
    diagonals = read(from_even.shape[0] - EXTRA + slot, 1)
    return faces, [unpack(body, diagonal) for body, diagonal in zip(bodies, diagonals)]


def assemble_kernel(members, has_base, *refs):
    links, half = refs[:2]
    base = refs[2] if has_base else None
    received = refs[2 + has_base : -5]
    norms, blocks, s_high, s_low, mixed = refs[-5:]
    slots = half.shape[0]
    top = None
    links = my_links(links, slots)
    for slot in range(slots):
        present, bit = links[slot]
        faces, diagonals = neighbour_parts(slot, bit, received, True)
        parts = [half[slot, 0]]
        parts += [present[k] * (half[slot, k] + 0.5 * turned(faces[k - 1])) for k in range(1, members)]
        parts += [present[k] * diagonals[k - 1] for k in range(1, members)]
        if has_base:
            for place in range(half.shape[1], len(parts)):
                parts[place] = parts[place] + base[slot, place]
        for place, part in enumerate(parts):
            blocks[slot, place] = part
        store_arrow((s_high, s_low), slot, parts)
    for slot in range(slots):
        total = None
        for row, col, block in square_blocks(s_high.at[slot], s_low.at[slot], mixed.at[slot]):
            part = jnp.sum(block * block, axis=0, keepdims=True)
            part = part if row == col else 2.0 * part
            total = part if total is None else total + part
        total = jnp.sum(total, axis=1, keepdims=True)
        top = total if top is None else jnp.maximum(top, total)
    norms[...] = jnp.broadcast_to(top.reshape(1, 1, 1), norms.shape)


def cube_kernel(blocks, out, s_high, s_low, q_high, q_low, mixed):
    slots, count = blocks.shape[:2]
    for slot in range(slots):
        parts = [blocks[slot, place] for place in range(count)]
        store_arrow((s_high, s_low), slot, parts)
        for place, part in enumerate(parts):
            out[slot, place] = part
    for slot in range(slots):
        for row, col, block in square_blocks(s_high.at[slot], s_low.at[slot], mixed.at[slot]):
            store_split((q_high, q_low), slot, span(row), span(col), block, row != col)
    for slot in range(slots):
        matrix = (s_high.at[slot], s_low.at[slot])
        square = (q_high.at[slot], q_low.at[slot])
        for place, (_, _, block) in enumerate(product_blocks(matrix, square)):
            out[slot, count + place] = block


def schedule(square, advance, slots, repeats):
    for repeat in range(repeats):
        for work in (square, advance):
            for slot in range(slots):
                for _ in work(slot, repeat):
                    pass


def sign_kernel(members, last, norms, source, own, *refs):
    targets = refs[:3]
    x, xh, xl, yh, yl, mixed = refs[3:]
    slots = source.shape[0]
    order = members * SIDE
    largest = jnp.max(norms[...], axis=0)
    scaling = 1.5 / jnp.sqrt(jnp.sqrt(largest + epsilon))
    linear = 1.5 * scaling
    cubic = -0.5 * (scaling * scaling * scaling)
    for slot in range(slots):
        for place, (row, col) in enumerate(PLACES):
            value = source[slot, 2 * members - 1 + place]
            value = cubic * (symmetric(value) if row == col else value)
            if row == col:
                value = value + linear * source[slot, members - 1 + row if row else 0]
            elif col == 0:
                value = value + linear * source[slot, row]
            elif row == 0:
                value = value + linear * turned(source[slot, col])
            x[slot, span(row), span(col)] = value
            store_split((xh.at[0], xl.at[0]), slot, span(row), span(col), value, row != col)

    def square(slot, repeat):
        iterate = (xh.at[repeat % 2, slot], xl.at[repeat % 2, slot])
        for row, col, block in square_blocks(*iterate, mixed.at[slot]):
            store_split((yh, yl), slot, span(row), span(col), block, row != col)
            yield

    def advance(slot, repeat):
        iterate = (xh.at[repeat % 2, slot], xl.at[repeat % 2, slot])
        target = (xh.at[1 - repeat % 2], xl.at[1 - repeat % 2])
        for row, col, block in product_blocks(iterate, (yh.at[slot], yl.at[slot])):
            at = (slot, span(row), span(col))
            value = 1.5 * x[at] - 0.5 * (symmetric(block) if row == col else block)
            x[at] = value
            store_split(target, *at, value, row != col)
            yield

    schedule(square, advance, slots, ITERS - 2)
    now = (ITERS - 2) % 2
    first = pl.ds(0, SIDE)

    def thin(slot, high, low):
        both = dot(jnp.concatenate([high, low], 0), xh[now, slot])
        return both[:SIDE] + both[SIDE:] + dot(high, xl[now, slot])

    middle = [thin(slot, xh[now, slot, first, :], xl[now, slot, first, :]) for slot in range(slots)]
    outer = [thin(slot, *split(middle[slot])) for slot in range(slots)]
    square = (SIDE, SIDE)
    eye = jnp.where(lanes(square) == rows_of(square), 0.5, 0.0)
    for slot in range(slots):
        parts = []
        for k in range(members):
            stored = x[slot, first, span(k)] if (0, k) in PLACES else turned(x[slot, span(k), first])
            parts.append(turned(0.25 * outer[slot][:, k * SIDE : (k + 1) * SIDE] - 0.75 * stored))
        parts[0] = symmetric(parts[0]) + eye
        fill_all(targets, slot, parts[1:], None if last else pack(parts[0]))
        for k in range(members):
            part = 0.5 * parts[k] if k else parts[0]
            own[slot, k] = part if last else part + source[slot, k]


def density_kernel(members, *refs):
    links, half = refs[:2]
    received = refs[2:-1]
    out = refs[-1]
    links = my_links(links, half.shape[0])
    for slot in range(half.shape[0]):
        present, bit = links[slot]
        faces, _ = neighbour_parts(slot, bit, received, False)
        out[slot, 0] = half[slot, 0]
        for k in range(1, members):
            out[slot, k] = present[k] * (half[slot, k] + 0.5 * turned(faces[k - 1]))


def exchange(over_even, over_odd, to_partner):
    cols = range(lax.axis_size("col"))
    rows = range(lax.axis_size("row"))
    odd = [(i, (i + 1 if i % 2 else i - 1) % len(cols)) for i in cols]
    received = [lax.ppermute(over_even, "col", [(i, i ^ 1) for i in cols])]
    received.append(lax.ppermute(over_odd, "col", odd))
    place = 1
    while place < len(rows):
        received.append(lax.ppermute(to_partner, "row", [(i, i ^ place) for i in rows]))
        place *= 2
    return received


def vmem():
    return pl.BlockSpec(memory_space=pltpu.VMEM)


def shape(*dims, dtype=f32):
    return jax.ShapeDtypeStruct(dims, dtype)


def call(kernel, name, operands, outputs, scratch=(), flops=0, smem_first=False):
    moved = sum(4 * a.size for a in (*operands, *outputs))
    specs = [vmem()] * len(operands)
    if smem_first:
        specs[0] = pl.BlockSpec(memory_space=pltpu.SMEM)
    return pl.pallas_call(
        kernel,
        out_shape=list(outputs),
        in_specs=specs,
        out_specs=[vmem()] * len(outputs),
        scratch_shapes=list(scratch),
        compiler_params=pltpu.CompilerParams(vmem_limit_bytes=24 * 1024 * 1024),
        cost_estimate=pl.CostEstimate(flops=flops, bytes_accessed=moved, transcendentals=0),
        name=name,
    )(*operands)


def per_device(hamiltonian, block_lists):
    slots, members = hamiltonian.shape[:2]
    order = members * SIDE
    cols = lax.axis_size("col")
    devices = lax.axis_size("row") * cols
    face = shape(message_rows(slots, False), SIDE)
    full = shape(message_rows(slots, True), SIDE)
    own = shape(slots, members, SIDE, SIDE)
    arrow = 2 * members - 1
    part_scratch = pltpu.VMEM((slots, order, order), bf16)
    both_scratch = pltpu.VMEM((2, slots, order, order), bf16)
    mixed_scratch = pltpu.VMEM((slots, order, order), f32)
    multiply = slots * 3 * 3 * order * order * order // 2

    half, *sent = call(pack_kernel, "pack", [hamiltonian], [own] + [full] * 3)
    (links,) = call(
        functools.partial(links_kernel, slots, cols),
        "links",
        [block_lists],
        [shape(slots * (members + 1), SIDE)],
        smem_first=True,
    )
    base = []
    for step in range(STEPS):
        last = step == STEPS - 1
        received = exchange(*sent)
        norms, blocks = call(
            functools.partial(assemble_kernel, members, len(base)),
            "assemble",
            [links, half, *base, *received],
            [shape(devices, 1, SIDE), shape(slots, arrow, SIDE, SIDE)],
            [part_scratch] * 2 + [mixed_scratch],
            flops=multiply,
        )
        norms = lax.all_to_all(norms, ("row", "col"), 0, 0, tiled=True)
        (source,) = call(
            cube_kernel,
            "cube",
            [blocks],
            [shape(slots, arrow + len(PLACES), SIDE, SIDE)],
            [part_scratch] * 4 + [mixed_scratch],
            flops=2 * multiply,
        )
        half, *sent = call(
            functools.partial(sign_kernel, members, last),
            "sign",
            [norms, source],
            [own] + [face if last else full] * 3,
            [pltpu.VMEM((slots, order, order), f32)] + [both_scratch] * 2 + [part_scratch] * 2 + [mixed_scratch],
            flops=8 * multiply,
        )
        base = [source]
    received = exchange(*sent)
    (density,) = call(
        functools.partial(density_kernel, members),
        "density",
        [links, half, *received],
        [own],
    )
    return density


def solution(mesh):
    return jax.shard_map(
        per_device,
        mesh=mesh,
        in_specs=(P(("row", "col"), None, None, None), P()),
        out_specs=P(("row", "col"), None, None, None),
        check_vma=False,
    )
```

```python
import functools
import jax
import jax.numpy as jnp
from jax import lax
from jax.experimental import pallas as pl
from jax.experimental.pallas import tpu as pltpu
from jax.sharding import PartitionSpec as P

ITERS = 6
STEPS = 2
SIDE = 128
HALF = SIDE // 2
EXTRA = 8

epsilon = 1e-06
f32 = jnp.float32
bf16 = jnp.bfloat16


def turned(block):
    return jnp.swapaxes(block, -1, -2)


def symmetric(block):
    return 0.5 * (block + turned(block))


def split(values):
    high = values.astype(bf16)
    return high, (values - high.astype(f32)).astype(bf16)


def dot(left, right):
    return lax.dot_general(left, right, (((1,), (0,)), ((), ())), preferred_element_type=f32)


def span(first, count=1):
    return pl.ds(first * SIDE, count * SIDE)


STRIPS = (((1, 3), (1, 2)), ((0,), (0, 1)), ((2,), (2, 0)), ((3,), (3, 0)))
PLACES = tuple((row, col) for rows, cols in STRIPS for row in rows for col in cols)


def block_rows(matrix, rows):
    return jnp.concatenate([matrix[span(row), :] for row in rows], 0)


def block_columns(matrix, cols):
    return jnp.concatenate([matrix[:, span(col)] for col in cols], 1)


def blocks_of(strip, rows, cols):
    for i, row in enumerate(rows):
        for j, col in enumerate(cols):
            yield row, col, strip[i * SIDE : (i + 1) * SIDE, j * SIDE : (j + 1) * SIDE]


def product_blocks(left, right):
    for rows, cols in STRIPS:
        high, low = block_rows(left[0], rows), block_rows(left[1], rows)
        right_high, right_low = block_columns(right[0], cols), block_columns(right[1], cols)
        both = dot(jnp.concatenate([high, low], 0), right_high)
        count = high.shape[0]
        yield from blocks_of(both[:count] + both[count:] + dot(high, right_low), rows, cols)


def square_blocks(high, low, mixed):
    for first in range(0, high.shape[0] // SIDE, 2):
        mixed[:, span(first, 2)] = dot(high[...], low[:, span(first, 2)])
    for rows, cols in STRIPS:
        strip = dot(block_rows(high, rows), block_columns(high, cols))
        for row, col, block in blocks_of(strip, rows, cols):
            yield row, col, block + (mixed[span(row), span(col)] + turned(mixed[span(col), span(row)]))


def store_split(target, slot, rows, columns, value, mirror):
    high, low = split(value)
    target[0][slot, rows, columns] = high
    target[1][slot, rows, columns] = low
    if mirror:
        high, low = split(turned(value))
        target[0][slot, columns, rows] = high
        target[1][slot, columns, rows] = low


def store_arrow(target, slot, blocks):
    members = (len(blocks) + 1) // 2
    empty = jnp.zeros((SIDE, SIDE), f32)
    for row in range(members):
        for col in range(members):
            if col == 0:
                value = blocks[row]
            elif row == 0:
                value = turned(blocks[col])
            elif row == col:
                value = blocks[members - 1 + row]
            else:
                value = empty
            at = (pl.ds(row * SIDE, SIDE), pl.ds(col * SIDE, SIDE))
            store_split(target, slot, *at, value, False)


def lanes(shape):
    return lax.broadcasted_iota(jnp.int32, shape, 1)


def rows_of(shape):
    return lax.broadcasted_iota(jnp.int32, shape, 0)


def pack(block):
    shape = (HALF, SIDE)
    lower = pltpu.roll(block[HALF:, :], HALF, 1)
    body = jnp.where(lanes(shape) < rows_of(shape), lower, block[:HALF, :])
    whole = block.shape
    return body, jnp.sum(jnp.where(lanes(whole) == rows_of(whole), block, 0.0), 0, keepdims=True)


def unpack(body, diagonal):
    shape = (HALF, SIDE)
    lane, row = lanes(shape), rows_of(shape)
    top = jnp.where(lane == row, 0.5 * body, jnp.where(lane < row, 0.0, body))
    rolled = pltpu.roll(body, HALF, 1)
    at = lane - HALF
    bottom = jnp.where(at == row, 0.5 * diagonal, jnp.where((at >= 0) & (at < row), rolled, 0.0))
    folded = jnp.concatenate([top, bottom], 0)
    return folded + turned(folded)


def message_rows(slots, with_diagonals):
    return slots * (SIDE + HALF) + EXTRA if with_diagonals else slots * SIDE


def fill(target, slot, face, packed):
    first = slot * (SIDE if packed is None else SIDE + HALF)
    target[pl.ds(first, SIDE), :] = face
    if packed is not None:
        body, diagonal = packed
        last = target.shape[0] - EXTRA
        target[pl.ds(first + SIDE, HALF), :] = body
        if slot == 0:
            target[pl.ds(last, EXTRA), :] = jnp.broadcast_to(diagonal, (EXTRA, SIDE))
        else:
            target[pl.ds(last + slot, 1), :] = diagonal


def fill_all(targets, slot, faces, packed):
    left, right, partner = faces
    even = lax.axis_index("col") % 2 == 0
    fill(targets[0], slot, jnp.where(even, right, left), packed)
    fill(targets[1], slot, jnp.where(even, left, right), packed)
    fill(targets[2], slot, partner, packed)


def pack_kernel(own, half, *targets):
    for slot in range(own.shape[0]):
        centre = symmetric(own[slot, 0])
        packed = pack(centre)
        half[slot, 0] = centre
        for k in range(1, own.shape[1]):
            half[slot, k] = 0.5 * own[slot, k]
        fill_all(targets, slot, [own[slot, k] for k in range(1, own.shape[1])], packed)


def links_kernel(slots, cols, lists, links):
    my_row = lax.axis_index("row")
    device = my_row * cols + lax.axis_index("col")
    count = links.shape[0] // slots
    for slot in range(slots):
        column = device * slots + slot
        partner_row = lists[column, 3] // (slots * cols)
        values = [jnp.where(lists[column, k] >= 0, 1.0, 0.0) for k in range(count - 1)]
        values.append(jnp.bitwise_xor(my_row, partner_row).astype(f32))
        for k, value in enumerate(values):
            links[pl.ds(slot * count + k, 1), :] = jnp.full((1, SIDE), value, f32)


def my_links(links, slots):
    count = links.shape[0] // slots
    rows = [links[pl.ds(place, 1), :] for place in range(slots * count)]
    return [(rows[slot * count : slot * count + count - 1], rows[slot * count + count - 1]) for slot in range(slots)]


def neighbour_parts(slot, bit, received, with_diagonals):
    from_even, from_odd = received[:2]
    from_rows = received[2:]
    even = lax.axis_index("col") % 2 == 0

    def read(first, count):
        part = pl.ds(first, count)
        partner = from_rows[0][part, :]
        for place in range(1, len(from_rows)):
            partner = jnp.where(bit == float(1 << place), from_rows[place][part, :], partner)
        near, far = from_even[part, :], from_odd[part, :]
        return jnp.where(even, far, near), jnp.where(even, near, far), partner

    start = slot * (SIDE + HALF if with_diagonals else SIDE)
    faces = read(start, SIDE)
    if not with_diagonals:
        return faces, None
    bodies = read(start + SIDE, HALF)
    diagonals = read(from_even.shape[0] - EXTRA + slot, 1)
    return faces, [unpack(body, diagonal) for body, diagonal in zip(bodies, diagonals)]


def assemble_kernel(members, has_base, *refs):
    links, half = refs[:2]
    base = refs[2] if has_base else None
    received = refs[2 + has_base : -5]
    norms, blocks, s_high, s_low, mixed = refs[-5:]
    slots = half.shape[0]
    top = None
    links = my_links(links, slots)
    for slot in range(slots):
        present, bit = links[slot]
        faces, diagonals = neighbour_parts(slot, bit, received, True)
        parts = [half[slot, 0]]
        parts += [present[k] * (half[slot, k] + 0.5 * turned(faces[k - 1])) for k in range(1, members)]
        parts += [present[k] * diagonals[k - 1] for k in range(1, members)]
        if has_base:
            parts = [part + base[slot, place] for place, part in enumerate(parts)]
        for place, part in enumerate(parts):
            blocks[slot, place] = part
        store_arrow((s_high, s_low), slot, parts)
    for slot in range(slots):
        total = None
        for row, col, block in square_blocks(s_high.at[slot], s_low.at[slot], mixed.at[slot]):
            part = jnp.sum(block * block, axis=0, keepdims=True)
            part = part if row == col else 2.0 * part
            total = part if total is None else total + part
        total = jnp.sum(total, axis=1, keepdims=True)
        top = total if top is None else jnp.maximum(top, total)
    norms[...] = jnp.broadcast_to(top.reshape(1, 1, 1), norms.shape)


def cube_kernel(blocks, out, s_high, s_low, q_high, q_low, mixed):
    slots, count = blocks.shape[:2]
    for slot in range(slots):
        parts = [blocks[slot, place] for place in range(count)]
        store_arrow((s_high, s_low), slot, parts)
        for place, part in enumerate(parts):
            out[slot, place] = part
    for slot in range(slots):
        for row, col, block in square_blocks(s_high.at[slot], s_low.at[slot], mixed.at[slot]):
            store_split((q_high, q_low), slot, span(row), span(col), block, row != col)
    for slot in range(slots):
        matrix = (s_high.at[slot], s_low.at[slot])
        square = (q_high.at[slot], q_low.at[slot])
        for place, (_, _, block) in enumerate(product_blocks(matrix, square)):
            out[slot, count + place] = block


def schedule(square, advance, slots, repeats):
    for repeat in range(repeats):
        for work in (square, advance):
            for slot in range(slots):
                for _ in work(slot, repeat):
                    pass


def sign_kernel(members, last, norms, source, own, *refs):
    targets = refs[:3]
    x, xh, xl, yh, yl, mixed = refs[3:]
    slots = source.shape[0]
    order = members * SIDE
    largest = jnp.max(norms[...], axis=0)
    scaling = 1.5 / jnp.sqrt(jnp.sqrt(largest + epsilon))
    linear = 1.5 * scaling
    cubic = -0.5 * (scaling * scaling * scaling)
    for slot in range(slots):
        for place, (row, col) in enumerate(PLACES):
            value = source[slot, 2 * members - 1 + place]
            value = cubic * (symmetric(value) if row == col else value)
            if row == col:
                value = value + linear * source[slot, members - 1 + row if row else 0]
            elif col == 0:
                value = value + linear * source[slot, row]
            elif row == 0:
                value = value + linear * turned(source[slot, col])
            x[slot, span(row), span(col)] = value
            store_split((xh.at[0], xl.at[0]), slot, span(row), span(col), value, row != col)

    def square(slot, repeat):
        iterate = (xh.at[repeat % 2, slot], xl.at[repeat % 2, slot])
        for row, col, block in square_blocks(*iterate, mixed.at[slot]):
            store_split((yh, yl), slot, span(row), span(col), block, row != col)
            yield

    def advance(slot, repeat):
        iterate = (xh.at[repeat % 2, slot], xl.at[repeat % 2, slot])
        target = (xh.at[1 - repeat % 2], xl.at[1 - repeat % 2])
        for row, col, block in product_blocks(iterate, (yh.at[slot], yl.at[slot])):
            at = (slot, span(row), span(col))
            value = 1.5 * x[at] - 0.5 * (symmetric(block) if row == col else block)
            x[at] = value
            store_split(target, *at, value, row != col)
            yield

    schedule(square, advance, slots, ITERS - 2)
    now = (ITERS - 2) % 2
    first = pl.ds(0, SIDE)

    def thin(slot, high, low):
        both = dot(jnp.concatenate([high, low], 0), xh[now, slot])
        return both[:SIDE] + both[SIDE:] + dot(high, xl[now, slot])

    middle = [thin(slot, xh[now, slot, first, :], xl[now, slot, first, :]) for slot in range(slots)]
    outer = [thin(slot, *split(middle[slot])) for slot in range(slots)]
    square = (SIDE, SIDE)
    eye = jnp.where(lanes(square) == rows_of(square), 0.5, 0.0)
    for slot in range(slots):
        parts = []
        for k in range(members):
            stored = x[slot, first, span(k)] if (0, k) in PLACES else turned(x[slot, span(k), first])
            parts.append(turned(0.25 * outer[slot][:, k * SIDE : (k + 1) * SIDE] - 0.75 * stored))
        parts[0] = symmetric(parts[0]) + eye
        fill_all(targets, slot, parts[1:], None if last else pack(parts[0]))
        own[slot, 0] = parts[0]
        for k in range(1, members):
            own[slot, k] = 0.5 * parts[k]


def density_kernel(members, *refs):
    links, half = refs[:2]
    received = refs[2:-1]
    out = refs[-1]
    links = my_links(links, half.shape[0])
    for slot in range(half.shape[0]):
        present, bit = links[slot]
        faces, _ = neighbour_parts(slot, bit, received, False)
        out[slot, 0] = half[slot, 0]
        for k in range(1, members):
            out[slot, k] = present[k] * (half[slot, k] + 0.5 * turned(faces[k - 1]))


def exchange(over_even, over_odd, to_partner):
    cols = range(lax.axis_size("col"))
    rows = range(lax.axis_size("row"))
    odd = [(i, (i + 1 if i % 2 else i - 1) % len(cols)) for i in cols]
    received = [lax.ppermute(over_even, "col", [(i, i ^ 1) for i in cols])]
    received.append(lax.ppermute(over_odd, "col", odd))
    place = 1
    while place < len(rows):
        received.append(lax.ppermute(to_partner, "row", [(i, i ^ place) for i in rows]))
        place *= 2
    return received


def vmem():
    return pl.BlockSpec(memory_space=pltpu.VMEM)


def shape(*dims, dtype=f32):
    return jax.ShapeDtypeStruct(dims, dtype)


def call(kernel, name, operands, outputs, scratch=(), flops=0, smem_first=False):
    moved = sum(4 * a.size for a in (*operands, *outputs))
    specs = [vmem()] * len(operands)
    if smem_first:
        specs[0] = pl.BlockSpec(memory_space=pltpu.SMEM)
    return pl.pallas_call(
        kernel,
        out_shape=list(outputs),
        in_specs=specs,
        out_specs=[vmem()] * len(outputs),
        scratch_shapes=list(scratch),
        compiler_params=pltpu.CompilerParams(vmem_limit_bytes=24 * 1024 * 1024),
        cost_estimate=pl.CostEstimate(flops=flops, bytes_accessed=moved, transcendentals=0),
        name=name,
    )(*operands)


def per_device(hamiltonian, block_lists):
    slots, members = hamiltonian.shape[:2]
    order = members * SIDE
    cols = lax.axis_size("col")
    devices = lax.axis_size("row") * cols
    face = shape(message_rows(slots, False), SIDE)
    full = shape(message_rows(slots, True), SIDE)
    own = shape(slots, members, SIDE, SIDE)
    arrow = 2 * members - 1
    part_scratch = pltpu.VMEM((slots, order, order), bf16)
    both_scratch = pltpu.VMEM((2, slots, order, order), bf16)
    mixed_scratch = pltpu.VMEM((slots, order, order), f32)
    multiply = slots * 3 * 3 * order * order * order // 2

    half, *sent = call(pack_kernel, "pack", [hamiltonian], [own] + [full] * 3)
    (links,) = call(
        functools.partial(links_kernel, slots, cols),
        "links",
        [block_lists],
        [shape(slots * (members + 1), SIDE)],
        smem_first=True,
    )
    base = []
    for step in range(STEPS):
        last = step == STEPS - 1
        received = exchange(*sent)
        norms, blocks = call(
            functools.partial(assemble_kernel, members, len(base)),
            "assemble",
            [links, half, *base, *received],
            [shape(devices, 1, SIDE), shape(slots, arrow, SIDE, SIDE)],
            [part_scratch] * 2 + [mixed_scratch],
            flops=multiply,
        )
        norms = lax.all_to_all(norms, ("row", "col"), 0, 0, tiled=True)
        (source,) = call(
            cube_kernel,
            "cube",
            [blocks],
            [shape(slots, arrow + len(PLACES), SIDE, SIDE)],
            [part_scratch] * 4 + [mixed_scratch],
            flops=2 * multiply,
        )
        half, *sent = call(
            functools.partial(sign_kernel, members, last),
            "sign",
            [norms, source],
            [own] + [face if last else full] * 3,
            [pltpu.VMEM((slots, order, order), f32)] + [both_scratch] * 2 + [part_scratch] * 2 + [mixed_scratch],
            flops=8 * multiply,
        )
        base = [source]
    received = exchange(*sent)
    (density,) = call(
        functools.partial(density_kernel, members),
        "density",
        [links, half, *received],
        [own],
    )
    return density


def solution(mesh):
    return jax.shard_map(
        per_device,
        mesh=mesh,
        in_specs=(P(("row", "col"), None, None, None), P()),
        out_specs=P(("row", "col"), None, None, None),
        check_vma=False,
    )
```
